32 devices in a mesh: batch: 8 (over z, core), mem: 4 (over y, x).
Axes of the slice: x: 2, y: 2, z: 4, core: 2. Of those that a mesh axis runs over, the one named last changes fastest.
Arguments:
- queries: bfloat16 [4096, 256], P(('mem', 'batch')), may hold values from -10 to 10
- positives: bfloat16 [4096, 256], P(('mem', 'batch')), may hold values from -0.25 to 0.25, as said below
- pos_ids: int32 [4096], replicated, may hold values from 0 to 31
- pos_logq: int32 [4096], replicated, may hold values from -10240 to -4097
- mem_items: bfloat16 [1024, 256], P(('batch', 'mem')), may hold values from -0.375 to 0.375
- mem_ids: int32 [1024], replicated, may hold values from 0 to 31
- mem_logq: int32 [1024], replicated, may hold values from -12288 to -6145
- mem_age: int32 [1024], replicated, may hold values from 0 to 23
- counts: int32 [512], replicated, may hold values from 1 to 64, 4096 in all
Outputs:
- row_loss: float32 [4096], P(('mem', 'batch'))
- query_grad: float32 [4096, 256], P(('mem', 'batch'))
- positive_grad: float32 [4096, 256], P(('mem', 'batch'))
The draws below stay inside these ranges and needn't reach their ends.
Inputs may be any that keep to these rules, and one draw needn't show every extreme that they name: `positives`: item embeddings. The counts sum to 4096; the largest is 64.
All inputs are finite; a program needn't handle non-finite values.
Results may differ from the reference program's by a relative error of at most 0.0033.
Values may be sent and summed in bfloat16 or wider, within the bound.
No kernel may reach another device: no remote copies, remote signals or barrier semaphores. Data moves between devices by JAX's collectives and lax.ppermute only.
A program may use at most 64 MiB of HBM per device.

```python
import math
import jax
import jax.numpy as jnp
import numpy as np
from jax import lax

D = 256
QB = 128
MEM_DEV = 32
MOST = 64
ITEMS = 32
AGE_LIMIT = 16
IMPS = 4096
MEM_ROWS = 1024
REQS = 512
N_BATCH = 8
N_MEM = 4


def positive_base(key):
    fresh_draw = jax.random.truncated_normal(jax.random.fold_in(key, 11), -4.0, 4.0, (IMPS, D), jnp.float32) / 16.0
    return fresh_draw


def draw_positives(key, part):
    return positive_base(key).astype(jnp.bfloat16)


def draw_queries(key, part):
    query_noise = jax.random.truncated_normal(jax.random.fold_in(key, 21), -4.0, 4.0, (IMPS, D), jnp.float32) * 0.25
    return query_noise.astype(jnp.bfloat16)


def with_ends(array, stream_key, smallest, top_value):
    longest = array.shape.index(max(array.shape))
    spots = []
    for shift in (0, 1):
        where = [jax.random.randint(jax.random.fold_in(stream_key, axis), (), 0, length) for axis, length in enumerate(array.shape)]
        where[longest] = (where[longest] + shift) % array.shape[longest]
        spots.append(tuple(where))
    return array.at[spots[0]].set(smallest).at[spots[1]].set(top_value)


def steps_of(key, shape, cuts, least, largest):
    level = 1.0
    for axis_at, blocks in cuts:
        steps = jax.random.uniform(jax.random.fold_in(jax.random.fold_in(key, 6), axis_at), (blocks,), jnp.float32, least / len(cuts), largest / len(cuts))
        level = level * jnp.repeat(jnp.exp(steps), shape[axis_at] // blocks).reshape((-1,) + (1,) * (len(shape) - 1 - axis_at))
    return level


def rank_table(count, lean):
    weights = [(1 << 20) // math.isqrt(standing ** lean) + 1 for standing in range(1, count + 1)]
    deviation = 1 + sum(weights) // (1 << 30)
    return np.cumsum(np.array([max(1, weight // deviation) for weight in weights]))


def ranked(stream_key, extent, number_of, lean):
    table = rank_table(number_of, lean)
    lot = jax.random.randint(jax.random.fold_in(stream_key, 1), extent, 0, int(table[number_of - 1]))
    grade = jnp.searchsorted(jnp.asarray(table, jnp.int32), lot, side="right")
    return jax.random.permutation(jax.random.fold_in(stream_key, 2), number_of)[grade].astype(jnp.int32)


def split_up(count, total, limit, lean):
    weights = [(1 << 20) // math.isqrt(standing ** lean) + 1 for standing in range(2, count + 1)]
    spare, holding = total - limit - (count - 1), [1] * (count - 1)
    while spare > 0:
        free = [i for i in range(count - 1) if holding[i] < limit]
        pool, budget = sum([weights[i] for i in free]), spare
        for i in free:
            extra = min(limit - holding[i], max(1, budget * weights[i] // pool), spare)
            holding[i] = holding[i] + extra
            spare = spare - extra
    return np.array([limit] + holding)


def ragged_sizes(rng, number_of, total, most, skew):
    if number_of == 2:
        one = jax.random.randint(rng, (), max(1, total - most), min(most, total - 1) + 1)
        return jnp.stack([one, total - one])
    tallies = jnp.asarray(split_up(number_of, total, most, skew), jnp.int32)
    couples = (number_of - 1) // 2
    donor, sink = tallies[1:1 + 2 * couples:2], tallies[2:2 + 2 * couples:2]
    margin = jnp.minimum(donor - 1, most - sink)
    shifted = jax.random.randint(jax.random.fold_in(rng, 1), (couples,), 0, 1 << 20) % (margin + 1)
    tallies = tallies.at[1:1 + 2 * couples:2].set(donor - shifted).at[2:2 + 2 * couples:2].set(sink + shifted)
    return tallies[jax.random.permutation(jax.random.fold_in(rng, 2), number_of)]


def centred(own_key, shape, scale, limit, pieces=(), kind=jnp.bfloat16):
    drawn = scale * jax.random.normal(own_key, shape, jnp.float32)
    if pieces:
        drawn = drawn * steps_of(own_key, shape, pieces, -0.22, 0.18)
    return jnp.clip(drawn, -limit, limit).astype(kind)


def setup_inputs(seed: int = 0) -> dict:
    key_of = jax.random.split(jax.random.key(seed), 10)
    return {
        "queries": draw_queries(jax.random.fold_in(key_of[9], 71), 0),
        "positives": draw_positives(jax.random.fold_in(key_of[9], 71), 0),
        "pos_ids": with_ends(ranked(key_of[2], (IMPS,), ITEMS, 2), jax.random.fold_in(key_of[2], 3), 0, ITEMS - 1).astype(jnp.int32),
        "pos_logq": with_ends(jax.random.randint(key_of[3], (IMPS,), -10240, -4096), jax.random.fold_in(key_of[3], 1), -10240, (-4096) - 1).astype(jnp.int32),
        "mem_items": centred(key_of[4], (MEM_ROWS, D), 0.0625, 0.375, ((0, 32),)),
        "mem_ids": with_ends(ranked(key_of[5], (MEM_ROWS,), ITEMS, 2), jax.random.fold_in(key_of[5], 3), 0, ITEMS - 1).astype(jnp.int32),
        "mem_logq": with_ends(jax.random.randint(key_of[6], (MEM_ROWS,), -12288, -6144), jax.random.fold_in(key_of[6], 1), -12288, (-6144) - 1).astype(jnp.int32),
        "mem_age": with_ends(jax.random.randint(key_of[7], (MEM_ROWS,), 0, 24), jax.random.fold_in(key_of[7], 1), 0, 23).astype(jnp.int32),
        "counts": ragged_sizes(key_of[8], REQS, IMPS, MOST, 2).astype(jnp.int32),
    }


inv_temp = 8.0
logq_unit = 1.0 / 1024.0


def request_of(counts, positions):
    req_ends = jnp.cumsum(counts)
    return jnp.searchsorted(req_ends, positions, side="right").astype(jnp.int32)


def scores(left_mat, right_mat):
    return lax.dot_general(left_mat, right_mat, (((1,), (1,)), ((), ())), preferred_element_type=jnp.float32)


def reference(queries, positives, pos_ids, pos_logq, mem_items, mem_ids, mem_logq, mem_age, counts):
    group_rows = QB * N_BATCH
    bank_rows = MEM_DEV * N_MEM
    row_index = jnp.arange(IMPS, dtype=jnp.int32)
    request = request_of(counts, row_index)
    weight = 1.0 / jnp.take(counts, request).astype(jnp.float32)
    pos_shift = -pos_logq.astype(jnp.float32) * logq_unit
    mem_shift = -mem_logq.astype(jnp.float32) * logq_unit
    mem_live = mem_age < AGE_LIMIT

    def one_block(grad_total, block_num):
        offset = block_num * QB
        group_first = (offset // group_rows) * group_rows
        bank_first = ((offset % group_rows) // QB) * bank_rows
        query_blk = lax.dynamic_slice_in_dim(queries, offset, QB, 0)
        own_rows = offset + jnp.arange(QB, dtype=jnp.int32)
        own_ids = lax.dynamic_slice_in_dim(pos_ids, offset, QB, 0)
        own_req = lax.dynamic_slice_in_dim(request, offset, QB, 0)
        own_weight = lax.dynamic_slice_in_dim(weight, offset, QB, 0)
        own_pos = lax.dynamic_slice_in_dim(positives, offset, QB, 0)
        own_shift = lax.dynamic_slice_in_dim(pos_shift, offset, QB, 0)
        cand_pos = lax.dynamic_slice_in_dim(positives, group_first, group_rows, 0)
        cand_rows = group_first + jnp.arange(group_rows, dtype=jnp.int32)
        cand_ids = lax.dynamic_slice_in_dim(pos_ids, group_first, group_rows, 0)
        cand_req = lax.dynamic_slice_in_dim(request, group_first, group_rows, 0)
        cand_shift = lax.dynamic_slice_in_dim(pos_shift, group_first, group_rows, 0)
        bank_items = lax.dynamic_slice_in_dim(mem_items, bank_first, bank_rows, 0)
        bank_ids = lax.dynamic_slice_in_dim(mem_ids, bank_first, bank_rows, 0)
        bank_shift = lax.dynamic_slice_in_dim(mem_shift, bank_first, bank_rows, 0)
        bank_live = lax.dynamic_slice_in_dim(mem_live, bank_first, bank_rows, 0)
        diagonal = cand_rows[None, :] == own_rows[:, None]
        keep_pos = diagonal | ((cand_ids[None, :] != own_ids[:, None]) & (cand_req[None, :] != own_req[:, None]))
        keep_mem = bank_live[None, :] & (bank_ids[None, :] != own_ids[:, None])
        pos_logit = inv_temp * scores(query_blk, cand_pos) + cand_shift[None, :]
        mem_logit = inv_temp * scores(query_blk, bank_items) + bank_shift[None, :]
        row_max = jnp.maximum(jnp.max(jnp.where(keep_pos, pos_logit, -jnp.inf), axis=1), jnp.max(jnp.where(keep_mem, mem_logit, -jnp.inf), axis=1))
        pos_exps = jnp.where(keep_pos, jnp.exp(jnp.where(keep_pos, pos_logit, row_max[:, None]) - row_max[:, None]), 0.0)
        mem_exps = jnp.where(keep_mem, jnp.exp(jnp.where(keep_mem, mem_logit, row_max[:, None]) - row_max[:, None]), 0.0)
        row_lse = row_max + jnp.log(jnp.sum(pos_exps, axis=1) + jnp.sum(mem_exps, axis=1))
        pos_prob = jnp.where(keep_pos, jnp.exp(jnp.where(keep_pos, pos_logit, row_lse[:, None]) - row_lse[:, None]), 0.0)
        mem_prob = jnp.where(keep_mem, jnp.exp(jnp.where(keep_mem, mem_logit, row_lse[:, None]) - row_lse[:, None]), 0.0)
        pos_coef = (own_weight[:, None] * pos_prob).astype(jnp.bfloat16)
        mem_coef = (own_weight[:, None] * mem_prob).astype(jnp.bfloat16)
        query_grad = inv_temp * (jnp.dot(pos_coef, cand_pos, preferred_element_type=jnp.float32) + jnp.dot(mem_coef, bank_items, preferred_element_type=jnp.float32)) - inv_temp * own_weight[:, None] * own_pos.astype(jnp.float32)
        column = inv_temp * lax.dot_general(pos_coef, query_blk, (((0,), (0,)), ((), ())), preferred_element_type=jnp.float32)
        current = lax.dynamic_slice_in_dim(grad_total, group_first, group_rows, 0)
        grad_total = lax.dynamic_update_slice_in_dim(grad_total, current + column, group_first, 0)
        own_logit = inv_temp * jnp.sum(query_blk.astype(jnp.float32) * own_pos.astype(jnp.float32), axis=1) + own_shift
        return grad_total, (row_lse - own_logit, query_grad)

    grad_start = jnp.zeros((IMPS, D), jnp.float32)
    pos_grad, (loss_blocks, query_blocks) = lax.scan(one_block, grad_start, jnp.arange(IMPS // QB, dtype=jnp.int32))
    positive_grad = pos_grad - inv_temp * weight[:, None] * queries.astype(jnp.float32)
    return loss_blocks.reshape(IMPS), query_blocks.reshape(IMPS, D), positive_grad
```

```python
import jax
import jax.numpy as jnp
from jax import lax
from jax.experimental import pallas as pl
from jax.experimental.pallas import tpu as pltpu
from jax.sharding import PartitionSpec as P

AGE_LIMIT = 16
inv_temp = 8.0
logq_unit = 1.0 / 1024.0
very_low = -1e30
LANES = 128
VMEM_LIMIT = 32 * 1024 * 1024


def nt_dot(left_mat, right_mat):
    return lax.dot_general(
        left_mat, right_mat, (((1,), (1,)), ((), ())), preferred_element_type=jnp.float32
    )


def tn_dot(left_mat, right_mat):
    return lax.dot_general(
        left_mat, right_mat, (((0,), (0,)), ((), ())), preferred_element_type=jnp.float32
    )


def as_column(row):
    return jnp.broadcast_to(row, (LANES, LANES)).T


def prep_kernel(n_batch, ids_ref, logq_ref, counts_ref, bias_ref, weight_ref, wcol_ref):
    own = lax.axis_index("batch")
    first_block = lax.axis_index("mem") * n_batch
    reqs = counts_ref.shape[0] * LANES
    sub = lax.broadcasted_iota(jnp.int32, (reqs, LANES), 0)
    lane = lax.broadcasted_iota(jnp.int32, (reqs, LANES), 1)
    ones = jnp.ones((LANES, LANES), jnp.bfloat16)
    ends = jnp.zeros((reqs, LANES), jnp.float32)
    for c in range(counts_ref.shape[0]):
        part = counts_ref[c : c + 1, :].astype(jnp.float32)
        tri = jnp.where(lane + c * LANES <= sub, part, 0.0).astype(jnp.bfloat16)
        ends = ends + jnp.dot(tri, ones, preferred_element_type=jnp.float32)
    ends = ends.astype(jnp.int32)
    sub = sub[:LANES]
    lane = lane[:LANES]
    rows = []
    for k in range(n_batch):
        block = first_block + jnp.bitwise_xor(own, k)
        pos = block * LANES + lane[:1]
        done = ends <= pos
        start = jnp.max(jnp.where(done, ends, 0), axis=0, keepdims=True)
        end = jnp.min(jnp.where(done, jnp.int32(2**30), ends), axis=0, keepdims=True)
        weight = 1.0 / (end - start).astype(jnp.float32)
        weight_ref[k : k + 1, :] = weight
        if k == 0:
            wcol_ref[...] = as_column(weight)
        rows.append((ids_ref[pl.ds(block, 1), :], start, end))
    for n in range(n_batch):
        block = first_block + jnp.bitwise_xor(own, n)
        id_col = as_column(ids_ref[pl.ds(block, 1), :])
        shift_col = as_column(-logq_ref[pl.ds(block, 1), :].astype(jnp.float32) * logq_unit)
        pos_col = block * LANES + sub
        for k in range(n_batch):
            id_row, start, end = rows[k]
            keep = (id_col != id_row) & ((pos_col < start) | (pos_col >= end))
            if n == k:
                keep = keep | (sub == lane)
            bias_ref[n * LANES : (n + 1) * LANES, k * LANES : (k + 1) * LANES] = jnp.where(
                keep, shift_col, very_low
            )


def bank_kernel(
    n_batch, pack_ref, s0, s1, s2, s3, ids_ref, mem_ids_ref, mem_logq_ref, mem_age_ref,
    bank_ref, logit_ref, lse_ref,
):
    own = lax.axis_index("batch")
    group = lax.axis_index("mem")
    slots = s0.shape[0]
    for k, shard in enumerate((s0, s1, s2, s3)):
        at = pl.multiple_of(jnp.bitwise_xor(group, k) * slots, slots)
        bank_ref[pl.ds(at, slots), :] = shard[...]
    id_row = ids_ref[pl.ds(group * n_batch + own, 1), :]
    id_col = as_column(mem_ids_ref[pl.ds(own, 1), :])
    shift_col = as_column(-mem_logq_ref[pl.ds(own, 1), :].astype(jnp.float32) * logq_unit)
    age_col = as_column(mem_age_ref[pl.ds(own, 1), :])
    keep = (age_col < AGE_LIMIT) & (id_col != id_row)
    logit = nt_dot(bank_ref[...], pack_ref[:LANES, :])
    logit = jnp.where(keep, logit + shift_col, very_low)
    top = jnp.max(logit, axis=0, keepdims=True)
    total = jnp.sum(jnp.exp(logit - top), axis=0, keepdims=True)
    logit_ref[...] = logit
    lse_ref[...] = top + jnp.log(total)


def main_kernel(n_batch, *refs):
    packs = refs[:n_batch]
    lses = refs[n_batch : 2 * n_batch]
    bias_ref, weight_ref, wcol_ref, bank_ref, mem_logit_ref = refs[2 * n_batch : 2 * n_batch + 5]
    loss_ref, qgrad_ref, pgrad_ref = refs[2 * n_batch + 5 : 2 * n_batch + 8]
    items, queries = refs[2 * n_batch + 8 :]
    for k in range(n_batch):
        queries[k * LANES : (k + 1) * LANES, :] = packs[k][:LANES, :]
        items[k * LANES : (k + 1) * LANES, :] = packs[k][LANES:, :]
    width = 2 * LANES
    pgrad = -wcol_ref[:, :1] * queries[:LANES, :].astype(jnp.float32)
    for c in range(n_batch // 2):
        at = slice(c * width, (c + 1) * width)
        q_part = queries[at, :]
        logit = nt_dot(items[...], q_part) + bias_ref[:, at]
        top = jnp.max(logit, axis=0, keepdims=True)
        total = jnp.sum(jnp.exp(logit - top), axis=0, keepdims=True)
        mem_lse = jnp.concatenate([lses[2 * c][...], lses[2 * c + 1][...]], axis=1)
        weight = jnp.concatenate(
            [weight_ref[2 * c : 2 * c + 1, :], weight_ref[2 * c + 1 : 2 * c + 2, :]], axis=1
        )
        high = jnp.maximum(top, mem_lse)
        lse = high + jnp.log(total * jnp.exp(top - high) + jnp.exp(mem_lse - high))
        coef = (weight * jnp.exp(logit[:LANES] - lse)).astype(jnp.bfloat16)
        pgrad = pgrad + jnp.dot(coef, q_part, preferred_element_type=jnp.float32)
        if c == 0:
            own_lse = lse[:, :LANES]
            own_weight = weight[:, :LANES]
            own = logit[:, :LANES]
            diag = lax.broadcasted_iota(jnp.int32, (LANES, LANES), 0) == (
                lax.broadcasted_iota(jnp.int32, (LANES, LANES), 1)
            )
            own_logit = jnp.sum(jnp.where(diag, own[:LANES], 0.0), axis=0, keepdims=True)
            loss_ref[...] = own_lse - own_logit
            row_coef = (own_weight * jnp.exp(own - own_lse)).astype(jnp.bfloat16)
            mem_coef = (own_weight * jnp.exp(mem_logit_ref[...] - own_lse)).astype(jnp.bfloat16)
            qgrad = tn_dot(row_coef, items[...]) + tn_dot(mem_coef, bank_ref[...])
            qgrad_ref[...] = inv_temp * (
                qgrad - wcol_ref[:, :1] * items[:LANES, :].astype(jnp.float32)
            )
    pgrad_ref[...] = pgrad


def in_vmem(count):
    return [pl.BlockSpec(memory_space=pltpu.VMEM)] * count


def call(kernel, outs, args, scratch=()):
    return pl.pallas_call(
        kernel,
        out_shape=outs,
        in_specs=in_vmem(len(args)),
        out_specs=in_vmem(len(outs)),
        scratch_shapes=list(scratch),
        compiler_params=pltpu.CompilerParams(vmem_limit_bytes=VMEM_LIMIT),
    )(*args)


def f32(*shape):
    return jax.ShapeDtypeStruct(shape, jnp.float32)


def swap(array, axis, mask):
    size = lax.axis_size(axis)
    return lax.ppermute(array, axis, [(s, s ^ mask) for s in range(size)])


def small_body(
    queries, positives, pos_ids, pos_logq, mem_items, mem_ids, mem_logq, mem_age, counts
):
    own_count, depth = queries.shape
    n_batch = lax.axis_size("batch")
    group_rows = own_count * n_batch
    ids = pos_ids.reshape(-1, LANES)
    logq = pos_logq.reshape(-1, LANES)
    banks = [a.reshape(-1, LANES) for a in (mem_ids, mem_logq, mem_age)]

    pack = jnp.concatenate([queries * jnp.bfloat16(inv_temp), positives], 0)
    far = swap(pack, "batch", 4)
    near = swap(pack, "batch", 2)
    shards = [mem_items] + [swap(mem_items, "mem", k) for k in (1, 2, 3)]
    bias, weight, wcol = call(
        lambda *r: prep_kernel(n_batch, *r),
        [f32(group_rows, group_rows), f32(n_batch, LANES), f32(LANES, LANES)],
        (ids, logq, counts.reshape(-1, LANES)),
    )
    bank, mem_logit, mem_lse = call(
        lambda *r: bank_kernel(n_batch, *r),
        [jax.ShapeDtypeStruct((LANES, depth), jnp.bfloat16), f32(LANES, LANES), f32(1, LANES)],
        (pack, *shards, ids, *banks),
    )
    packs = {0: pack, 4: far, 2: near, 6: swap(far, "batch", 2)}
    lses = {0: mem_lse}
    for k in (4, 6, 2):
        lses[k] = swap(mem_lse, "batch", k)
    for k in (0, 2, 4, 6):
        packs[k + 1] = swap(packs[k], "batch", 1)
        lses[k + 1] = swap(lses[k], "batch", 1)
    order = range(n_batch)
    loss, query_grad, positive_grad = call(
        lambda *r: main_kernel(n_batch, *r),
        [f32(1, LANES), f32(own_count, depth), f32(own_count, depth)],
        (
            *[packs[k] for k in order],
            *[lses[k] for k in order],
            bias,
            weight,
            wcol,
            bank,
            mem_logit,
        ),
        [pltpu.VMEM((group_rows, depth), jnp.bfloat16)] * 2,
    )
    return loss.reshape(own_count), query_grad, positive_grad


def request_span(counts, positions):
    ends = jnp.cumsum(counts)
    which = jnp.searchsorted(ends, positions, side="right")
    return which, jnp.take(counts, which)


def masked_exp(tile_logits, level):
    return jnp.where(tile_logits > very_low, jnp.exp(tile_logits - level[:, None]), 0.0)


def large_body(
    queries, positives, pos_ids, pos_logq, mem_items, mem_ids, mem_logq, mem_age, counts
):
    own_count = queries.shape[0]
    group_rows = own_count * lax.axis_size("batch")
    bank_rows = mem_items.shape[0] * lax.axis_size("mem")
    batch_index = lax.axis_index("batch")
    group_first = lax.axis_index("mem") * group_rows
    own_first = group_first + batch_index * own_count
    bank_first = batch_index * bank_rows

    def part(array, first, size):
        return lax.dynamic_slice_in_dim(array, first, size, 0)

    def shift_of(array, first, size):
        return -part(array, first, size).astype(jnp.float32) * logq_unit

    own_rows = own_first + jnp.arange(own_count, dtype=jnp.int32)
    col_rows = group_first + jnp.arange(group_rows, dtype=jnp.int32)
    own_req, own_size = request_span(counts, own_rows)
    weight = 1.0 / own_size.astype(jnp.float32)
    cand_req, _ = request_span(counts, col_rows)
    own_ids = part(pos_ids, own_first, own_count)
    cand_ids = part(pos_ids, group_first, group_rows)
    bank_ids = part(mem_ids, bank_first, bank_rows)
    bank_live = part(mem_age, bank_first, bank_rows) < AGE_LIMIT
    bank_items = lax.all_gather(mem_items, "mem", axis=0, tiled=True)
    mem_mask = bank_live[None, :] & (bank_ids[None, :] != own_ids[:, None])
    mem_logits = jnp.where(
        mem_mask,
        inv_temp * nt_dot(queries, bank_items) + shift_of(mem_logq, bank_first, bank_rows)[None, :],
        very_low,
    )
    group_items = lax.all_gather(positives, "batch", axis=0, tiled=True)
    kept = (col_rows[None, :] == own_rows[:, None]) | (
        cand_ids[None, :] != own_ids[:, None]
    ) & (cand_req[None, :] != own_req[:, None])
    logits = jnp.where(
        kept,
        inv_temp * nt_dot(queries, group_items)
        + shift_of(pos_logq, group_first, group_rows)[None, :],
        very_low,
    )
    row_max = jnp.maximum(jnp.max(logits, axis=1), jnp.max(mem_logits, axis=1))
    row_lse = row_max + jnp.log(
        jnp.sum(masked_exp(logits, row_max), axis=1)
        + jnp.sum(masked_exp(mem_logits, row_max), axis=1)
    )
    pos_coef = (weight[:, None] * masked_exp(logits, row_lse)).astype(jnp.bfloat16)
    mem_coef = (weight[:, None] * masked_exp(mem_logits, row_lse)).astype(jnp.bfloat16)
    own_term = inv_temp * weight[:, None]
    query_grad = inv_temp * (
        jnp.dot(pos_coef, group_items, preferred_element_type=jnp.float32)
        + jnp.dot(mem_coef, bank_items, preferred_element_type=jnp.float32)
    ) - own_term * positives.astype(jnp.float32)
    column_share = lax.psum_scatter(
        inv_temp * tn_dot(pos_coef, queries), "batch", scatter_dimension=0, tiled=True
    )
    wide_q = queries.astype(jnp.float32)
    own_logit = inv_temp * jnp.sum(wide_q * positives.astype(jnp.float32), axis=1) + shift_of(
        pos_logq, own_first, own_count
    )
    return row_lse - own_logit, query_grad, column_share - own_term * wide_q


def solution(mesh):
    small = mesh.shape["batch"] == 8 and mesh.shape["mem"] == 4
    own = P(("mem", "batch"), None)
    in_specs = (own, own, P(), P(), P(("batch", "mem"), None), P(), P(), P(), P())
    out_specs = (P(("mem", "batch")), own, own)
    return jax.shard_map(
        small_body if small else large_body,
        mesh=mesh,
        in_specs=in_specs,
        out_specs=out_specs,
        check_vma=False,
    )
```

```python
import jax
import jax.numpy as jnp
from jax import lax
from jax.experimental import pallas as pl
from jax.experimental.pallas import tpu as pltpu
from jax.sharding import PartitionSpec as P

AGE_LIMIT = 16
inv_temp = 8.0
logq_unit = 1.0 / 1024.0
very_low = -1e30
LANES = 128
VMEM_LIMIT = 32 * 1024 * 1024


def nt_dot(left_mat, right_mat):
    return lax.dot_general(
        left_mat, right_mat, (((1,), (1,)), ((), ())), preferred_element_type=jnp.float32
    )


def tn_dot(left_mat, right_mat):
    return lax.dot_general(
        left_mat, right_mat, (((0,), (0,)), ((), ())), preferred_element_type=jnp.float32
    )


def as_column(row):
    return jnp.broadcast_to(row, (LANES, LANES)).T


def fetch(pairs, sems):
    copies = [pltpu.make_async_copy(src, dst, sems.at[k]) for k, (src, dst) in enumerate(pairs)]
    for copy in copies:
        copy.start()
    for copy in copies:
        copy.wait()


def prep_kernel(
    n_batch, ids_hbm, logq_hbm, counts_hbm, mem_ids_hbm, mem_logq_hbm, mem_age_hbm,
    bias_ref, weight_ref, wcol_ref, mem_bias_ref,
    ids_ref, logq_ref, counts_ref, mem_ids_ref, mem_logq_ref, mem_age_ref, sems,
):
    fetch(
        [
            (ids_hbm, ids_ref),
            (logq_hbm, logq_ref),
            (counts_hbm, counts_ref),
            (mem_ids_hbm, mem_ids_ref),
            (mem_logq_hbm, mem_logq_ref),
            (mem_age_hbm, mem_age_ref),
        ],
        sems,
    )
    own = lax.axis_index("batch")
    first_block = lax.axis_index("mem") * n_batch
    reqs = counts_ref.shape[0] * LANES
    sub = lax.broadcasted_iota(jnp.int32, (reqs, LANES), 0)
    lane = lax.broadcasted_iota(jnp.int32, (reqs, LANES), 1)
    ones = jnp.ones((LANES, LANES), jnp.bfloat16)
    ends = jnp.zeros((reqs, LANES), jnp.float32)
    for c in range(counts_ref.shape[0]):
        part = counts_ref[c : c + 1, :].astype(jnp.float32)
        tri = jnp.where(lane + c * LANES <= sub, part, 0.0).astype(jnp.bfloat16)
        ends = ends + jnp.dot(tri, ones, preferred_element_type=jnp.float32)
    ends = ends.astype(jnp.int32)
    sub = sub[:LANES]
    lane = lane[:LANES]
    rows = []
    for k in range(n_batch):
        block = first_block + jnp.bitwise_xor(own, k)
        pos = block * LANES + lane[:1]
        done = ends <= pos
        start = jnp.max(jnp.where(done, ends, 0), axis=0, keepdims=True)
        end = jnp.min(jnp.where(done, jnp.int32(2**30), ends), axis=0, keepdims=True)
        weight = 1.0 / (end - start).astype(jnp.float32)
        weight_ref[k : k + 1, :] = weight
        if k == 0:
            wcol_ref[...] = as_column(weight)
        rows.append((ids_ref[pl.ds(block, 1), :], start, end))
    id_col = as_column(mem_ids_ref[pl.ds(own, 1), :])
    shift_col = as_column(-mem_logq_ref[pl.ds(own, 1), :].astype(jnp.float32) * logq_unit)
    age_col = as_column(mem_age_ref[pl.ds(own, 1), :])
    keep = (age_col < AGE_LIMIT) & (id_col != rows[0][0])
    mem_bias_ref[...] = jnp.where(keep, shift_col, very_low)
    for n in range(n_batch):
        block = first_block + jnp.bitwise_xor(own, n)
        id_col = as_column(ids_ref[pl.ds(block, 1), :])
        shift_col = as_column(-logq_ref[pl.ds(block, 1), :].astype(jnp.float32) * logq_unit)
        pos_col = block * LANES + sub
        for k in range(n_batch):
            id_row, start, end = rows[k]
            keep = (id_col != id_row) & ((pos_col < start) | (pos_col >= end))
            if n == k:
                keep = keep | (sub == lane)
            bias_ref[n * LANES : (n + 1) * LANES, k * LANES : (k + 1) * LANES] = jnp.where(
                keep, shift_col, very_low
            )


def bank_kernel(
    q_hbm, s0_hbm, s1, s2, s3, mem_bias_ref, bank_ref, logit_ref, lse_ref, q_ref, s0, sems
):
    fetch([(q_hbm, q_ref), (s0_hbm, s0)], sems)
    group = lax.axis_index("mem")
    slots = s0.shape[0]
    for k, shard in enumerate((s0, s1, s2, s3)):
        at = pl.multiple_of(jnp.bitwise_xor(group, k) * slots, slots)
        bank_ref[pl.ds(at, slots), :] = shard[...]
    logit = inv_temp * nt_dot(bank_ref[...], q_ref[...]) + mem_bias_ref[...]
    top = jnp.max(logit, axis=0, keepdims=True)
    total = jnp.sum(jnp.exp(logit - top), axis=0, keepdims=True)
    logit_ref[...] = logit
    lse_ref[...] = top + jnp.log(total)


def stack_kernel(*refs):
    for k, ref in enumerate(refs[:-1]):
        refs[-1][k : k + 1, :] = ref[...]


def main_kernel(n_batch, *refs):
    p_refs = refs[:n_batch]
    q_refs = refs[n_batch : 2 * n_batch]
    rest = refs[2 * n_batch :]
    even_ref, odd_ref, bias_ref, weight_ref, wcol_ref, bank_ref, mem_logit_ref = rest[:7]
    loss_ref, qgrad_ref, pgrad_ref, items, queries, sems = rest[7:]
    own_rows = pl.ds(0, LANES)
    fetch([(p_refs[0], items.at[own_rows]), (q_refs[0], queries.at[own_rows])], sems)
    queries[:LANES, :] = queries[:LANES, :] * jnp.bfloat16(inv_temp)
    for k in range(1, n_batch):
        queries[k * LANES : (k + 1) * LANES, :] = q_refs[k][...] * jnp.bfloat16(inv_temp)
        items[k * LANES : (k + 1) * LANES, :] = p_refs[k][...]
    width = 2 * LANES
    pgrad = -wcol_ref[:, :1] * queries[:LANES, :].astype(jnp.float32)
    for c in range(n_batch // 2):
        at = slice(c * width, (c + 1) * width)
        q_part = queries[at, :]
        logit = nt_dot(items[...], q_part) + bias_ref[:, at]
        top = jnp.max(logit, axis=0, keepdims=True)
        total = jnp.sum(jnp.exp(logit - top), axis=0, keepdims=True)
        mem_lse = jnp.concatenate([even_ref[c : c + 1, :], odd_ref[c : c + 1, :]], axis=1)
        weight = jnp.concatenate(
            [weight_ref[2 * c : 2 * c + 1, :], weight_ref[2 * c + 1 : 2 * c + 2, :]], axis=1
        )
        high = jnp.maximum(top, mem_lse)
        lse = high + jnp.log(total * jnp.exp(top - high) + jnp.exp(mem_lse - high))
        coef = (weight * jnp.exp(logit[:LANES] - lse)).astype(jnp.bfloat16)
        pgrad = pgrad + jnp.dot(coef, q_part, preferred_element_type=jnp.float32)
        if c == 0:
            own_lse = lse[:, :LANES]
            own_weight = weight[:, :LANES]
            own = logit[:, :LANES]
            diag = lax.broadcasted_iota(jnp.int32, (LANES, LANES), 0) == (
                lax.broadcasted_iota(jnp.int32, (LANES, LANES), 1)
            )
            own_logit = jnp.sum(jnp.where(diag, own[:LANES], 0.0), axis=0, keepdims=True)
            loss_ref[...] = own_lse - own_logit
            row_coef = (own_weight * jnp.exp(own - own_lse)).astype(jnp.bfloat16)
            mem_coef = (own_weight * jnp.exp(mem_logit_ref[...] - own_lse)).astype(jnp.bfloat16)
            qgrad = tn_dot(row_coef, items[...]) + tn_dot(mem_coef, bank_ref[...])
            qgrad_ref[...] = inv_temp * (
                qgrad - wcol_ref[:, :1] * items[:LANES, :].astype(jnp.float32)
            )
    pgrad_ref[...] = pgrad


def call(kernel, outs, args, hbm=(), scratch=(), cost_us=1):
    in_vmem = pl.BlockSpec(memory_space=pltpu.VMEM)
    in_hbm = pl.BlockSpec(memory_space=pltpu.HBM)
    return pl.pallas_call(
        kernel,
        out_shape=outs,
        in_specs=[in_hbm if k in hbm else in_vmem for k in range(len(args))],
        out_specs=[in_vmem] * len(outs),
        scratch_shapes=list(scratch),
        compiler_params=pltpu.CompilerParams(vmem_limit_bytes=VMEM_LIMIT),
        cost_estimate=pl.CostEstimate(
            flops=int(cost_us * 1e9), bytes_accessed=int(cost_us * 3e6), transcendentals=0
        ),
    )(*args)


def f32(*shape):
    return jax.ShapeDtypeStruct(shape, jnp.float32)


def bf16(*shape):
    return jax.ShapeDtypeStruct(shape, jnp.bfloat16)


def swap(array, axis, mask):
    size = lax.axis_size(axis)
    return lax.ppermute(array, axis, [(s, s ^ mask) for s in range(size)])


def after(array, *others):
    return lax.optimization_barrier((array, *others))[0]


def small_body(
    queries, positives, pos_ids, pos_logq, mem_items, mem_ids, mem_logq, mem_age, counts
):
    own_count, depth = queries.shape
    n_batch = lax.axis_size("batch")
    group_rows = own_count * n_batch
    ints = [
        a.reshape(-1, LANES) for a in (pos_ids, pos_logq, counts, mem_ids, mem_logq, mem_age)
    ]

    p, q = {0: positives}, {0: queries}
    p[4] = swap(positives, "batch", 4)
    q[4] = swap(queries, "batch", 4)
    shards = [mem_items] + [swap(mem_items, "mem", k) for k in (1, 2, 3)]
    bias, weight, wcol, mem_bias = call(
        lambda *r: prep_kernel(n_batch, *r),
        [f32(group_rows, group_rows), f32(n_batch, LANES), f32(LANES, LANES), f32(LANES, LANES)],
        ints,
        hbm=range(len(ints)),
        scratch=[pltpu.VMEM(a.shape, jnp.int32) for a in ints]
        + [pltpu.SemaphoreType.DMA((len(ints),))],
        cost_us=3,
    )
    bank, mem_logit, lse = call(
        bank_kernel,
        [bf16(LANES, depth), f32(LANES, LANES), f32(1, LANES)],
        (queries, *shards, mem_bias),
        hbm=(0, 1),
        scratch=[
            pltpu.VMEM(queries.shape, jnp.bfloat16),
            pltpu.VMEM(mem_items.shape, jnp.bfloat16),
            pltpu.SemaphoreType.DMA((2,)),
        ],
    )
    p[6] = swap(p[4], "batch", 2)
    p[2] = swap(after(positives, lse), "batch", 2)
    q[6] = swap(q[4], "batch", 2)
    q[2] = swap(after(queries, lse), "batch", 2)
    lses = [lse] + [swap(lse, "batch", k) for k in (2, 4, 6)]
    (even,) = call(stack_kernel, [f32(4, LANES)], lses)
    odd = swap(even, "batch", 1)
    for k in (0, 2, 4, 6):
        for d in (p, q):
            d[k + 1] = swap(after(d[k], lse) if k == 0 else d[k], "batch", 1)
    order = range(n_batch)
    loss, query_grad, positive_grad = call(
        lambda *r: main_kernel(n_batch, *r),
        [f32(1, LANES), f32(own_count, depth), f32(own_count, depth)],
        (
            *[p[k] for k in order],
            *[q[k] for k in order],
            even,
            odd,
            bias,
            weight,
            wcol,
            bank,
            mem_logit,
        ),
        hbm=(0, n_batch),
        scratch=[pltpu.VMEM((group_rows, depth), jnp.bfloat16)] * 2
        + [pltpu.SemaphoreType.DMA((2,))],
        cost_us=3,
    )
    return loss.reshape(own_count), query_grad, positive_grad


def request_span(counts, positions):
    ends = jnp.cumsum(counts)
    which = jnp.searchsorted(ends, positions, side="right")
    return which, jnp.take(counts, which)


def masked_exp(tile_logits, level):
    return jnp.where(tile_logits > very_low, jnp.exp(tile_logits - level[:, None]), 0.0)


def large_body(
    queries, positives, pos_ids, pos_logq, mem_items, mem_ids, mem_logq, mem_age, counts
):
    own_count = queries.shape[0]
    group_rows = own_count * lax.axis_size("batch")
    bank_rows = mem_items.shape[0] * lax.axis_size("mem")
    batch_index = lax.axis_index("batch")
    group_first = lax.axis_index("mem") * group_rows
    own_first = group_first + batch_index * own_count
    bank_first = batch_index * bank_rows

    def part(array, first, size):
        return lax.dynamic_slice_in_dim(array, first, size, 0)

    def shift_of(array, first, size):
        return -part(array, first, size).astype(jnp.float32) * logq_unit

    own_rows = own_first + jnp.arange(own_count, dtype=jnp.int32)
    col_rows = group_first + jnp.arange(group_rows, dtype=jnp.int32)
    own_req, own_size = request_span(counts, own_rows)
    weight = 1.0 / own_size.astype(jnp.float32)
    cand_req, _ = request_span(counts, col_rows)
    own_ids = part(pos_ids, own_first, own_count)
    cand_ids = part(pos_ids, group_first, group_rows)
    bank_ids = part(mem_ids, bank_first, bank_rows)
    bank_live = part(mem_age, bank_first, bank_rows) < AGE_LIMIT
    bank_items = lax.all_gather(mem_items, "mem", axis=0, tiled=True)
    mem_mask = bank_live[None, :] & (bank_ids[None, :] != own_ids[:, None])
    mem_logits = jnp.where(
        mem_mask,
        inv_temp * nt_dot(queries, bank_items) + shift_of(mem_logq, bank_first, bank_rows)[None, :],
        very_low,
    )
    group_items = lax.all_gather(positives, "batch", axis=0, tiled=True)
    kept = (col_rows[None, :] == own_rows[:, None]) | (
        cand_ids[None, :] != own_ids[:, None]
    ) & (cand_req[None, :] != own_req[:, None])
    logits = jnp.where(
        kept,
        inv_temp * nt_dot(queries, group_items)
        + shift_of(pos_logq, group_first, group_rows)[None, :],
        very_low,
    )
    row_max = jnp.maximum(jnp.max(logits, axis=1), jnp.max(mem_logits, axis=1))
    row_lse = row_max + jnp.log(
        jnp.sum(masked_exp(logits, row_max), axis=1)
        + jnp.sum(masked_exp(mem_logits, row_max), axis=1)
    )
    pos_coef = (weight[:, None] * masked_exp(logits, row_lse)).astype(jnp.bfloat16)
    mem_coef = (weight[:, None] * masked_exp(mem_logits, row_lse)).astype(jnp.bfloat16)
    own_term = inv_temp * weight[:, None]
    query_grad = inv_temp * (
        jnp.dot(pos_coef, group_items, preferred_element_type=jnp.float32)
        + jnp.dot(mem_coef, bank_items, preferred_element_type=jnp.float32)
    ) - own_term * positives.astype(jnp.float32)
    column_share = lax.psum_scatter(
        inv_temp * tn_dot(pos_coef, queries), "batch", scatter_dimension=0, tiled=True
    )
    wide_q = queries.astype(jnp.float32)
    own_logit = inv_temp * jnp.sum(wide_q * positives.astype(jnp.float32), axis=1) + shift_of(
        pos_logq, own_first, own_count
    )
    return row_lse - own_logit, query_grad, column_share - own_term * wide_q


def solution(mesh):
    small = mesh.shape["batch"] == 8 and mesh.shape["mem"] == 4
    own = P(("mem", "batch"), None)
    in_specs = (own, own, P(), P(), P(("batch", "mem"), None), P(), P(), P(), P())
    out_specs = (P(("mem", "batch")), own, own)
    return jax.shard_map(
        small_body if small else large_body,
        mesh=mesh,
        in_specs=in_specs,
        out_specs=out_specs,
        check_vma=False,
    )
```

```python
import jax
import jax.numpy as jnp
from jax import lax
from jax.experimental import pallas as pl
from jax.experimental.pallas import tpu as pltpu
from jax.sharding import PartitionSpec as P

AGE_LIMIT = 16
inv_temp = 8.0
logq_unit = 1.0 / 1024.0
very_low = -1e30
LANES = 128
VMEM_LIMIT = 32 * 1024 * 1024


def nt_dot(left_mat, right_mat):
    return lax.dot_general(
        left_mat, right_mat, (((1,), (1,)), ((), ())), preferred_element_type=jnp.float32
    )


def tn_dot(left_mat, right_mat):
    return lax.dot_general(
        left_mat, right_mat, (((0,), (0,)), ((), ())), preferred_element_type=jnp.float32
    )


def as_column(row):
    return jnp.broadcast_to(row, (LANES, LANES)).T


def fetch(pairs, sems):
    copies = [pltpu.make_async_copy(src, dst, sems.at[k]) for k, (src, dst) in enumerate(pairs)]
    for copy in copies:
        copy.start()
    for copy in copies:
        copy.wait()


def pack_kernel(count, *refs):
    ins, outs = refs[: count + 2], refs[count + 2 : 2 * count + 3]
    q_ref, sems = refs[-2:]
    pack_ref = outs[-1]
    rows = q_ref.shape[0]
    fetch([*zip(ins[:count], outs[:count]), (ins[count], q_ref), (ins[count + 1], pack_ref.at[pl.ds(rows, rows)])], sems)
    pack_ref[:rows, :] = q_ref[...] * jnp.bfloat16(inv_temp)


def prep_kernel(
    n_batch, ids_ref, logq_ref, counts_ref, mem_ids_ref, mem_logq_ref, mem_age_ref,
    bias_ref, weight_ref, wcol_ref, mem_bias_ref,
):
    own = lax.axis_index("batch")
    first_block = lax.axis_index("mem") * n_batch
    reqs = counts_ref.shape[0] * LANES
    sub = lax.broadcasted_iota(jnp.int32, (reqs, LANES), 0)
    lane = lax.broadcasted_iota(jnp.int32, (reqs, LANES), 1)
    ones = jnp.ones((LANES, LANES), jnp.bfloat16)
    ends = jnp.zeros((reqs, LANES), jnp.float32)
    for c in range(counts_ref.shape[0]):
        part = counts_ref[c : c + 1, :].astype(jnp.float32)
        tri = jnp.where(lane + c * LANES <= sub, part, 0.0).astype(jnp.bfloat16)
        ends = ends + jnp.dot(tri, ones, preferred_element_type=jnp.float32)
    ends = ends.astype(jnp.int32)
    sub = sub[:LANES]
    lane = lane[:LANES]
    rows = []
    for k in range(n_batch):
        block = first_block + jnp.bitwise_xor(own, k)
        pos = block * LANES + lane[:1]
        done = ends <= pos
        start = jnp.max(jnp.where(done, ends, 0), axis=0, keepdims=True)
        end = jnp.min(jnp.where(done, jnp.int32(2**30), ends), axis=0, keepdims=True)
        weight = 1.0 / (end - start).astype(jnp.float32)
        weight_ref[k : k + 1, :] = weight
        if k == 0:
            wcol_ref[...] = as_column(weight)
        rows.append((ids_ref[pl.ds(block, 1), :], start, end))
    id_col = as_column(mem_ids_ref[pl.ds(own, 1), :])
    shift_col = as_column(-mem_logq_ref[pl.ds(own, 1), :].astype(jnp.float32) * logq_unit)
    age_col = as_column(mem_age_ref[pl.ds(own, 1), :])
    keep = (age_col < AGE_LIMIT) & (id_col != rows[0][0])
    mem_bias_ref[...] = jnp.where(keep, shift_col, very_low)
    for n in range(n_batch):
        block = first_block + jnp.bitwise_xor(own, n)
        id_col = as_column(ids_ref[pl.ds(block, 1), :])
        shift_col = as_column(-logq_ref[pl.ds(block, 1), :].astype(jnp.float32) * logq_unit)
        pos_col = block * LANES + sub
        for k in range(n_batch):
            id_row, start, end = rows[k]
            keep = (id_col != id_row) & ((pos_col < start) | (pos_col >= end))
            if n == k:
                keep = keep | (sub == lane)
            bias_ref[n * LANES : (n + 1) * LANES, k * LANES : (k + 1) * LANES] = jnp.where(
                keep, shift_col, very_low
            )


def bank_kernel(pack_ref, s0, s1, s2, s3, mem_bias_ref, bank_ref, logit_ref, lse_ref):
    group = lax.axis_index("mem")
    slots = s0.shape[0]
    for k, shard in enumerate((s0, s1, s2, s3)):
        at = pl.multiple_of(jnp.bitwise_xor(group, k) * slots, slots)
        bank_ref[pl.ds(at, slots), :] = shard[...]
    logit = nt_dot(bank_ref[...], pack_ref[:LANES, :]) + mem_bias_ref[...]
    top = jnp.max(logit, axis=0, keepdims=True)
    total = jnp.sum(jnp.exp(logit - top), axis=0, keepdims=True)
    logit_ref[...] = logit
    lse_ref[...] = top + jnp.log(total)


def stack_kernel(*refs):
    first = 0
    for ref in refs[:-1]:
        refs[-1][first : first + ref.shape[0], :] = ref[...]
        first += ref.shape[0]


def main_kernel(n_batch, *refs):
    evens = refs[: n_batch // 2]
    odd_ref, odd_last_ref = refs[n_batch // 2 : n_batch // 2 + 2]
    rest = refs[n_batch // 2 + 2 :]
    even_ref, odd_lse_ref, bias_ref, weight_ref, wcol_ref, bank_ref, mem_logit_ref = rest[:7]
    loss_ref, qgrad_ref, pgrad_ref, items, queries = rest[7:]
    block = evens[0].shape[0]
    for k in range(n_batch // 2):
        odd = odd_last_ref if k == n_batch // 2 - 1 else odd_ref.at[pl.ds(k * block, block)]
        for parity, ref in enumerate((evens[k], odd)):
            at = (2 * k + parity) * LANES
            queries[at : at + LANES, :] = ref[:LANES, :]
            items[at : at + LANES, :] = ref[LANES:, :]
    width = 2 * LANES
    pgrad = -wcol_ref[:, :1] * queries[:LANES, :].astype(jnp.float32)
    for c in range(n_batch // 2):
        at = slice(c * width, (c + 1) * width)
        q_part = queries[at, :]
        logit = nt_dot(items[...], q_part) + bias_ref[:, at]
        top = jnp.max(logit, axis=0, keepdims=True)
        total = jnp.sum(jnp.exp(logit - top), axis=0, keepdims=True)
        mem_lse = jnp.concatenate([even_ref[c : c + 1, :], odd_lse_ref[c : c + 1, :]], axis=1)
        weight = jnp.concatenate(
            [weight_ref[2 * c : 2 * c + 1, :], weight_ref[2 * c + 1 : 2 * c + 2, :]], axis=1
        )
        high = jnp.maximum(top, mem_lse)
        lse = high + jnp.log(total * jnp.exp(top - high) + jnp.exp(mem_lse - high))
        coef = (weight * jnp.exp(logit[:LANES] - lse)).astype(jnp.bfloat16)
        pgrad = pgrad + jnp.dot(coef, q_part, preferred_element_type=jnp.float32)
        if c == 0:
            own_lse = lse[:, :LANES]
            own_weight = weight[:, :LANES]
            own = logit[:, :LANES]
            diag = lax.broadcasted_iota(jnp.int32, (LANES, LANES), 0) == (
                lax.broadcasted_iota(jnp.int32, (LANES, LANES), 1)
            )
            own_logit = jnp.sum(jnp.where(diag, own[:LANES], 0.0), axis=0, keepdims=True)
            loss_ref[...] = own_lse - own_logit
            row_coef = (own_weight * jnp.exp(own - own_lse)).astype(jnp.bfloat16)
            mem_coef = (own_weight * jnp.exp(mem_logit_ref[...] - own_lse)).astype(jnp.bfloat16)
            qgrad = tn_dot(row_coef, items[...]) + tn_dot(mem_coef, bank_ref[...])
            qgrad_ref[...] = inv_temp * (
                qgrad - wcol_ref[:, :1] * items[:LANES, :].astype(jnp.float32)
            )
    pgrad_ref[...] = pgrad


def call(kernel, outs, args, hbm=(), scratch=(), cost_us=1):
    in_vmem = pl.BlockSpec(memory_space=pltpu.VMEM)
    in_hbm = pl.BlockSpec(memory_space=pltpu.HBM)
    args = [
        pltpu.with_memory_space_constraint(a, pltpu.HBM) if k in hbm else a
        for k, a in enumerate(args)
    ]
    return pl.pallas_call(
        kernel,
        out_shape=outs,
        in_specs=[in_hbm if k in hbm else in_vmem for k in range(len(args))],
        out_specs=[in_vmem] * len(outs),
        scratch_shapes=list(scratch),
        compiler_params=pltpu.CompilerParams(vmem_limit_bytes=VMEM_LIMIT),
        cost_estimate=pl.CostEstimate(
            flops=int(cost_us * 1e9), bytes_accessed=int(cost_us * 3e6), transcendentals=0
        ),
    )(*args)


def f32(*shape):
    return jax.ShapeDtypeStruct(shape, jnp.float32)


def bf16(*shape):
    return jax.ShapeDtypeStruct(shape, jnp.bfloat16)


def swap(array, axis, mask):
    size = lax.axis_size(axis)
    return lax.ppermute(array, axis, [(s, s ^ mask) for s in range(size)])


def after(array, *others):
    return lax.optimization_barrier((array, *others))[0]


def small_body(
    queries, positives, pos_ids, pos_logq, mem_items, mem_ids, mem_logq, mem_age, counts
):
    own_count, depth = queries.shape
    n_batch = lax.axis_size("batch")
    group_rows = own_count * n_batch
    ints = [
        a.reshape(-1, LANES) for a in (pos_ids, pos_logq, counts, mem_ids, mem_logq, mem_age)
    ]

    small = (*ints, mem_items)
    *ints, shard, pack = call(
        lambda *r: pack_kernel(len(small), *r),
        [jax.ShapeDtypeStruct(a.shape, a.dtype) for a in small] + [bf16(2 * own_count, depth)],
        (*small, queries, positives),
        hbm=range(len(small) + 2),
        scratch=[
            pltpu.VMEM(queries.shape, queries.dtype),
            pltpu.SemaphoreType.DMA((len(small) + 2,)),
        ],
    )
    far = swap(pack, "batch", 4)
    shards = [shard] + [swap(shard, "mem", k) for k in (1, 2, 3)]
    near = swap(pack, "batch", 2)
    bias, weight, wcol, mem_bias = call(
        lambda *r: prep_kernel(n_batch, *r),
        [f32(group_rows, group_rows), f32(n_batch, LANES), f32(LANES, LANES), f32(LANES, LANES)],
        ints,
        cost_us=3,
    )
    bank, mem_logit, lse = call(
        bank_kernel,
        [bf16(LANES, depth), f32(LANES, LANES), f32(1, LANES)],
        (pack, *shards, mem_bias),
    )
    last = swap(after(far, lse), "batch", 2)
    lses = [lse] + [swap(lse, "batch", k) for k in (2, 4, 6)]
    (even,) = call(stack_kernel, [f32(4, LANES)], lses)
    odd = swap(even, "batch", 1)
    (early,) = call(stack_kernel, [bf16(6 * own_count, depth)], (pack, near, far))
    odd_early = swap(early, "batch", 1)
    odd_last = swap(after(last, *lses), "batch", 1)
    loss, query_grad, positive_grad = call(
        lambda *r: main_kernel(n_batch, *r),
        [f32(1, LANES), f32(own_count, depth), f32(own_count, depth)],
        (pack, near, far, last, odd_early, odd_last)
        + (even, odd, bias, weight, wcol, bank, mem_logit),
        scratch=[pltpu.VMEM((group_rows, depth), jnp.bfloat16)] * 2,
        cost_us=3,
    )
    return loss.reshape(own_count), query_grad, positive_grad


def request_span(counts, positions):
    ends = jnp.cumsum(counts)
    which = jnp.searchsorted(ends, positions, side="right")
    return which, jnp.take(counts, which)


def masked_exp(tile_logits, level):
    return jnp.where(tile_logits > very_low, jnp.exp(tile_logits - level[:, None]), 0.0)


def large_body(
    queries, positives, pos_ids, pos_logq, mem_items, mem_ids, mem_logq, mem_age, counts
):
    own_count = queries.shape[0]
    group_rows = own_count * lax.axis_size("batch")
    bank_rows = mem_items.shape[0] * lax.axis_size("mem")
    batch_index = lax.axis_index("batch")
    group_first = lax.axis_index("mem") * group_rows
    own_first = group_first + batch_index * own_count
    bank_first = batch_index * bank_rows

    def part(array, first, size):
        return lax.dynamic_slice_in_dim(array, first, size, 0)

    def shift_of(array, first, size):
        return -part(array, first, size).astype(jnp.float32) * logq_unit

    own_rows = own_first + jnp.arange(own_count, dtype=jnp.int32)
    col_rows = group_first + jnp.arange(group_rows, dtype=jnp.int32)
    own_req, own_size = request_span(counts, own_rows)
    weight = 1.0 / own_size.astype(jnp.float32)
    cand_req, _ = request_span(counts, col_rows)
    own_ids = part(pos_ids, own_first, own_count)
    cand_ids = part(pos_ids, group_first, group_rows)
    bank_ids = part(mem_ids, bank_first, bank_rows)
    bank_live = part(mem_age, bank_first, bank_rows) < AGE_LIMIT
    bank_items = lax.all_gather(mem_items, "mem", axis=0, tiled=True)
    mem_mask = bank_live[None, :] & (bank_ids[None, :] != own_ids[:, None])
    mem_logits = jnp.where(
        mem_mask,
        inv_temp * nt_dot(queries, bank_items) + shift_of(mem_logq, bank_first, bank_rows)[None, :],
        very_low,
    )
    group_items = lax.all_gather(positives, "batch", axis=0, tiled=True)
    kept = (col_rows[None, :] == own_rows[:, None]) | (
        cand_ids[None, :] != own_ids[:, None]
    ) & (cand_req[None, :] != own_req[:, None])
    logits = jnp.where(
        kept,
        inv_temp * nt_dot(queries, group_items)
        + shift_of(pos_logq, group_first, group_rows)[None, :],
        very_low,
    )
    row_max = jnp.maximum(jnp.max(logits, axis=1), jnp.max(mem_logits, axis=1))
    row_lse = row_max + jnp.log(
        jnp.sum(masked_exp(logits, row_max), axis=1)
        + jnp.sum(masked_exp(mem_logits, row_max), axis=1)
    )
    pos_coef = (weight[:, None] * masked_exp(logits, row_lse)).astype(jnp.bfloat16)
    mem_coef = (weight[:, None] * masked_exp(mem_logits, row_lse)).astype(jnp.bfloat16)
    own_term = inv_temp * weight[:, None]
    query_grad = inv_temp * (
        jnp.dot(pos_coef, group_items, preferred_element_type=jnp.float32)
        + jnp.dot(mem_coef, bank_items, preferred_element_type=jnp.float32)
    ) - own_term * positives.astype(jnp.float32)
    column_share = lax.psum_scatter(
        inv_temp * tn_dot(pos_coef, queries), "batch", scatter_dimension=0, tiled=True
    )
    wide_q = queries.astype(jnp.float32)
    own_logit = inv_temp * jnp.sum(wide_q * positives.astype(jnp.float32), axis=1) + shift_of(
        pos_logq, own_first, own_count
    )
    return row_lse - own_logit, query_grad, column_share - own_term * wide_q


def solution(mesh):
    small = mesh.shape["batch"] == 8 and mesh.shape["mem"] == 4
    own = P(("mem", "batch"), None)
    in_specs = (own, own, P(), P(), P(("batch", "mem"), None), P(), P(), P(), P())
    out_specs = (P(("mem", "batch")), own, own)
    return jax.shard_map(
        small_body if small else large_body,
        mesh=mesh,
        in_specs=in_specs,
        out_specs=out_specs,
        check_vma=False,
    )
```

```python
import jax
import jax.numpy as jnp
from jax import lax
from jax.experimental import pallas as pl
from jax.experimental.pallas import tpu as pltpu
from jax.sharding import PartitionSpec as P

AGE_LIMIT = 16
inv_temp = 8.0
logq_unit = 1.0 / 1024.0
very_low = -1e30
LANES = 128
VMEM_LIMIT = 32 * 1024 * 1024


def nt_dot(left_mat, right_mat):
    return lax.dot_general(
        left_mat, right_mat, (((1,), (1,)), ((), ())), preferred_element_type=jnp.float32
    )


def tn_dot(left_mat, right_mat):
    return lax.dot_general(
        left_mat, right_mat, (((0,), (0,)), ((), ())), preferred_element_type=jnp.float32
    )


def as_column(row):
    return jnp.broadcast_to(row, (LANES, LANES)).T


def fetch(pairs, sems):
    copies = [pltpu.make_async_copy(src, dst, sems.at[k]) for k, (src, dst) in enumerate(pairs)]
    for copy in copies:
        copy.start()
    for copy in copies:
        copy.wait()


def pack_kernel(count, *refs):
    ins, outs = refs[: count + 2], refs[count + 2 : 2 * count + 3]
    q_ref, sems = refs[-2:]
    pack_ref = outs[-1]
    rows = q_ref.shape[0]
    pairs = [*zip(ins[:count], outs[:count])]
    pairs += [(ins[count], q_ref), (ins[count + 1], pack_ref.at[pl.ds(rows, rows)])]
    fetch(pairs, sems)
    pack_ref[:rows, :] = q_ref[...] * jnp.bfloat16(inv_temp)


def prep_kernel(
    n_batch, ids_ref, logq_ref, counts_ref, bias_ref, weight_ref, wcol_ref
):
    own = lax.axis_index("batch")
    first_block = lax.axis_index("mem") * n_batch
    reqs = counts_ref.shape[0] * LANES
    sub = lax.broadcasted_iota(jnp.int32, (reqs, LANES), 0)
    lane = lax.broadcasted_iota(jnp.int32, (reqs, LANES), 1)
    ones = jnp.ones((LANES, LANES), jnp.bfloat16)
    ends = jnp.zeros((reqs, LANES), jnp.float32)
    for c in range(counts_ref.shape[0]):
        part = counts_ref[c : c + 1, :].astype(jnp.float32)
        tri = jnp.where(lane + c * LANES <= sub, part, 0.0).astype(jnp.bfloat16)
        ends = ends + jnp.dot(tri, ones, preferred_element_type=jnp.float32)
    ends = ends.astype(jnp.int32)
    sub = sub[:LANES]
    lane = lane[:LANES]
    rows = []
    for k in range(n_batch):
        block = first_block + jnp.bitwise_xor(own, k)
        pos = block * LANES + lane[:1]
        done = ends <= pos
        start = jnp.max(jnp.where(done, ends, 0), axis=0, keepdims=True)
        end = jnp.min(jnp.where(done, jnp.int32(2**30), ends), axis=0, keepdims=True)
        weight = 1.0 / (end - start).astype(jnp.float32)
        weight_ref[k : k + 1, :] = weight
        if k == 0:
            wcol_ref[...] = as_column(weight)
        rows.append((ids_ref[pl.ds(block, 1), :], start))
    for n in range(n_batch):
        block = first_block + jnp.bitwise_xor(own, n)
        id_col, start_col = as_column(rows[n][0]), as_column(rows[n][1])
        shift_col = as_column(-logq_ref[pl.ds(block, 1), :].astype(jnp.float32) * logq_unit)
        for k in range(n_batch):
            id_row, start = rows[k]
            keep = (id_col != id_row) & (start_col != start)
            if n == k:
                keep = keep | (sub == lane)
            bias_ref[n * LANES : (n + 1) * LANES, k * LANES : (k + 1) * LANES] = jnp.where(
                keep, shift_col, very_low
            )


def bank_kernel(
    n_batch, pack_ref, s0, s1, s2, s3, ids_ref, mem_ids_ref, mem_logq_ref, mem_age_ref,
    bank_ref, logit_ref, lse_ref,
):
    own = lax.axis_index("batch")
    group = lax.axis_index("mem")
    slots = s0.shape[0]
    for k, shard in enumerate((s0, s1, s2, s3)):
        at = pl.multiple_of(jnp.bitwise_xor(group, k) * slots, slots)
        bank_ref[pl.ds(at, slots), :] = shard[...]
    id_row = ids_ref[pl.ds(group * n_batch + own, 1), :]
    id_col = as_column(mem_ids_ref[pl.ds(own, 1), :])
    shift_col = as_column(-mem_logq_ref[pl.ds(own, 1), :].astype(jnp.float32) * logq_unit)
    age_col = as_column(mem_age_ref[pl.ds(own, 1), :])
    keep = (age_col < AGE_LIMIT) & (id_col != id_row)
    bias = jnp.where(keep, shift_col, very_low)
    logit = nt_dot(bank_ref[...], pack_ref[:LANES, :]) + bias
    top = jnp.max(logit, axis=0, keepdims=True)
    total = jnp.sum(jnp.exp(logit - top), axis=0, keepdims=True)
    logit_ref[...] = logit
    lse_ref[...] = top + jnp.log(total)


def stack_kernel(*refs):
    first = 0
    for ref in refs[:-1]:
        refs[-1][first : first + ref.shape[0], :] = ref[...]
        first += ref.shape[0]


def main_kernel(n_batch, *refs):
    evens = refs[: n_batch // 2]
    odd_ref, odd_last_ref = refs[n_batch // 2 : n_batch // 2 + 2]
    rest = refs[n_batch // 2 + 2 :]
    even_ref, odd_lse_ref, bias_ref, weight_ref, wcol_ref, bank_ref, mem_logit_ref = rest[:7]
    loss_ref, qgrad_ref, pgrad_ref, items, queries = rest[7:]
    block = evens[0].shape[0]
    for k in range(n_batch // 2):
        odd = odd_last_ref if k == n_batch // 2 - 1 else odd_ref.at[pl.ds(k * block, block)]
        for parity, ref in enumerate((evens[k], odd)):
            at = (2 * k + parity) * LANES
            queries[at : at + LANES, :] = ref[:LANES, :]
            items[at : at + LANES, :] = ref[LANES:, :]
    width = 2 * LANES
    pgrad = -wcol_ref[:, :1] * queries[:LANES, :].astype(jnp.float32)
    for c in range(n_batch // 2):
        at = slice(c * width, (c + 1) * width)
        q_part = queries[at, :]
        logit = nt_dot(items[...], q_part) + bias_ref[:, at]
        top = jnp.max(logit, axis=0, keepdims=True)
        total = jnp.sum(jnp.exp(logit - top), axis=0, keepdims=True)
        mem_lse = jnp.concatenate([even_ref[c : c + 1, :], odd_lse_ref[c : c + 1, :]], axis=1)
        weight = jnp.concatenate(
            [weight_ref[2 * c : 2 * c + 1, :], weight_ref[2 * c + 1 : 2 * c + 2, :]], axis=1
        )
        high = jnp.maximum(top, mem_lse)
        lse = high + jnp.log(total * jnp.exp(top - high) + jnp.exp(mem_lse - high))
        coef = (weight * jnp.exp(logit[:LANES] - lse)).astype(jnp.bfloat16)
        pgrad = pgrad + jnp.dot(coef, q_part, preferred_element_type=jnp.float32)
        if c == 0:
            own_lse = lse[:, :LANES]
            own_weight = weight[:, :LANES]
            own = logit[:, :LANES]
            diag = lax.broadcasted_iota(jnp.int32, (LANES, LANES), 0) == (
                lax.broadcasted_iota(jnp.int32, (LANES, LANES), 1)
            )
            own_logit = jnp.sum(jnp.where(diag, own[:LANES], 0.0), axis=0, keepdims=True)
            loss_ref[...] = own_lse - own_logit
            row_coef = (own_weight * jnp.exp(own - own_lse)).astype(jnp.bfloat16)
            mem_coef = (own_weight * jnp.exp(mem_logit_ref[...] - own_lse)).astype(jnp.bfloat16)
            qgrad = tn_dot(row_coef, items[...]) + tn_dot(mem_coef, bank_ref[...])
            qgrad_ref[...] = inv_temp * (
                qgrad - wcol_ref[:, :1] * items[:LANES, :].astype(jnp.float32)
            )
    pgrad_ref[...] = pgrad


def call(kernel, outs, args, hbm=(), scratch=(), cost_us=1):
    in_vmem = pl.BlockSpec(memory_space=pltpu.VMEM)
    in_hbm = pl.BlockSpec(memory_space=pltpu.HBM)
    args = [
        pltpu.with_memory_space_constraint(a, pltpu.HBM) if k in hbm else a
        for k, a in enumerate(args)
    ]
    return pl.pallas_call(
        kernel,
        out_shape=outs,
        in_specs=[in_hbm if k in hbm else in_vmem for k in range(len(args))],
        out_specs=[in_vmem] * len(outs),
        scratch_shapes=list(scratch),
        compiler_params=pltpu.CompilerParams(vmem_limit_bytes=VMEM_LIMIT),
        cost_estimate=pl.CostEstimate(
            flops=int(cost_us * 1e9), bytes_accessed=int(cost_us * 3e6), transcendentals=0
        ),
    )(*args)


def f32(*shape):
    return jax.ShapeDtypeStruct(shape, jnp.float32)


def bf16(*shape):
    return jax.ShapeDtypeStruct(shape, jnp.bfloat16)


def swap(array, axis, mask):
    size = lax.axis_size(axis)
    return lax.ppermute(array, axis, [(s, s ^ mask) for s in range(size)])


def after(array, *others):
    return lax.optimization_barrier((array, *others))[0]


def small_body(
    queries, positives, pos_ids, pos_logq, mem_items, mem_ids, mem_logq, mem_age, counts
):
    own_count, depth = queries.shape
    n_batch = lax.axis_size("batch")
    group_rows = own_count * n_batch
    ints = [
        a.reshape(-1, LANES) for a in (pos_ids, pos_logq, counts, mem_ids, mem_logq, mem_age)
    ]

    small = (*ints, mem_items)
    *ints, shard, pack = call(
        lambda *r: pack_kernel(len(small), *r),
        [jax.ShapeDtypeStruct(a.shape, a.dtype) for a in small] + [bf16(2 * own_count, depth)],
        (*small, queries, positives),
        hbm=range(len(small) + 2),
        scratch=[
            pltpu.VMEM(queries.shape, queries.dtype),
            pltpu.SemaphoreType.DMA((len(small) + 2,)),
        ],
    )
    far = swap(pack, "batch", 4)
    near = swap(pack, "batch", 2)
    shards = [shard] + [swap(shard, "mem", k) for k in (1, 2, 3)]
    bias, weight, wcol = call(
        lambda *r: prep_kernel(n_batch, *r),
        [f32(group_rows, group_rows), f32(n_batch, LANES), f32(LANES, LANES)],
        ints[:3],
        cost_us=3,
    )
    bank, mem_logit, lse = call(
        lambda *r: bank_kernel(n_batch, *r),
        [bf16(LANES, depth), f32(LANES, LANES), f32(1, LANES)],
        (pack, *shards, ints[0], *ints[3:]),
    )
    last = swap(far, "batch", 2)
    (even,) = call(
        stack_kernel, [f32(4, LANES)], [lse] + [swap(lse, "batch", k) for k in (2, 4, 6)]
    )
    odd = swap(after(even, weight), "batch", 1)
    (early,) = call(stack_kernel, [bf16(6 * own_count, depth)], (pack, near, far))
    odd_early = swap(early, "batch", 1)
    odd_last = swap(last, "batch", 1)
    loss, query_grad, positive_grad = call(
        lambda *r: main_kernel(n_batch, *r),
        [f32(1, LANES), f32(own_count, depth), f32(own_count, depth)],
        (pack, near, far, last, odd_early, odd_last)
        + (even, odd, bias, weight, wcol, bank, mem_logit),
        scratch=[pltpu.VMEM((group_rows, depth), jnp.bfloat16)] * 2,
        cost_us=3,
    )
    return loss.reshape(own_count), query_grad, positive_grad


def request_span(counts, positions):
    ends = jnp.cumsum(counts)
    which = jnp.searchsorted(ends, positions, side="right")
    return which, jnp.take(counts, which)


def masked_exp(tile_logits, level):
    return jnp.where(tile_logits > very_low, jnp.exp(tile_logits - level[:, None]), 0.0)


def large_body(
    queries, positives, pos_ids, pos_logq, mem_items, mem_ids, mem_logq, mem_age, counts
):
    own_count = queries.shape[0]
    group_rows = own_count * lax.axis_size("batch")
    bank_rows = mem_items.shape[0] * lax.axis_size("mem")
    batch_index = lax.axis_index("batch")
    group_first = lax.axis_index("mem") * group_rows
    own_first = group_first + batch_index * own_count
    bank_first = batch_index * bank_rows

    def part(array, first, size):
        return lax.dynamic_slice_in_dim(array, first, size, 0)

    def shift_of(array, first, size):
        return -part(array, first, size).astype(jnp.float32) * logq_unit

    own_rows = own_first + jnp.arange(own_count, dtype=jnp.int32)
    col_rows = group_first + jnp.arange(group_rows, dtype=jnp.int32)
    own_req, own_size = request_span(counts, own_rows)
    weight = 1.0 / own_size.astype(jnp.float32)
    cand_req, _ = request_span(counts, col_rows)
    own_ids = part(pos_ids, own_first, own_count)
    cand_ids = part(pos_ids, group_first, group_rows)
    bank_ids = part(mem_ids, bank_first, bank_rows)
    bank_live = part(mem_age, bank_first, bank_rows) < AGE_LIMIT
    bank_items = lax.all_gather(mem_items, "mem", axis=0, tiled=True)
    mem_mask = bank_live[None, :] & (bank_ids[None, :] != own_ids[:, None])
    mem_logits = jnp.where(
        mem_mask,
        inv_temp * nt_dot(queries, bank_items) + shift_of(mem_logq, bank_first, bank_rows)[None, :],
        very_low,
    )
    group_items = lax.all_gather(positives, "batch", axis=0, tiled=True)
    kept = (col_rows[None, :] == own_rows[:, None]) | (
        cand_ids[None, :] != own_ids[:, None]
    ) & (cand_req[None, :] != own_req[:, None])
    logits = jnp.where(
        kept,
        inv_temp * nt_dot(queries, group_items)
        + shift_of(pos_logq, group_first, group_rows)[None, :],
        very_low,
    )
    row_max = jnp.maximum(jnp.max(logits, axis=1), jnp.max(mem_logits, axis=1))
    row_lse = row_max + jnp.log(
        jnp.sum(masked_exp(logits, row_max), axis=1)
        + jnp.sum(masked_exp(mem_logits, row_max), axis=1)
    )
    pos_coef = (weight[:, None] * masked_exp(logits, row_lse)).astype(jnp.bfloat16)
    mem_coef = (weight[:, None] * masked_exp(mem_logits, row_lse)).astype(jnp.bfloat16)
    own_term = inv_temp * weight[:, None]
    query_grad = inv_temp * (
        jnp.dot(pos_coef, group_items, preferred_element_type=jnp.float32)
        + jnp.dot(mem_coef, bank_items, preferred_element_type=jnp.float32)
    ) - own_term * positives.astype(jnp.float32)
    column_share = lax.psum_scatter(
        inv_temp * tn_dot(pos_coef, queries), "batch", scatter_dimension=0, tiled=True
    )
    wide_q = queries.astype(jnp.float32)
    own_logit = inv_temp * jnp.sum(wide_q * positives.astype(jnp.float32), axis=1) + shift_of(
        pos_logq, own_first, own_count
    )
    return row_lse - own_logit, query_grad, column_share - own_term * wide_q


def solution(mesh):
    small = mesh.shape["batch"] == 8 and mesh.shape["mem"] == 4
    own = P(("mem", "batch"), None)
    in_specs = (own, own, P(), P(), P(("batch", "mem"), None), P(), P(), P(), P())
    out_specs = (P(("mem", "batch")), own, own)
    return jax.shard_map(
        small_body if small else large_body,
        mesh=mesh,
        in_specs=in_specs,
        out_specs=out_specs,
        check_vma=False,
    )
```

```python
import jax
import jax.numpy as jnp
from jax import lax
from jax.experimental import pallas as pl
from jax.experimental.pallas import tpu as pltpu
from jax.sharding import PartitionSpec as P

AGE_LIMIT = 16
inv_temp = 8.0
logq_unit = 1.0 / 1024.0
very_low = -1e30
LANES = 128
VMEM_LIMIT = 32 * 1024 * 1024
BANK_ORDER = (3, 1, 2)
SUM_ORDER = (6, 4, 2)


def nt_dot(left_mat, right_mat):
    return lax.dot_general(
        left_mat, right_mat, (((1,), (1,)), ((), ())), preferred_element_type=jnp.float32
    )


def tn_dot(left_mat, right_mat):
    return lax.dot_general(
        left_mat, right_mat, (((0,), (0,)), ((), ())), preferred_element_type=jnp.float32
    )


def as_column(row):
    return jnp.broadcast_to(row, (LANES, LANES)).T


def fetch(pairs, sems):
    copies = [pltpu.make_async_copy(src, dst, sems.at[k]) for k, (src, dst) in enumerate(pairs)]
    for copy in copies:
        copy.start()
    for copy in copies:
        copy.wait()


def pack_kernel(count, *refs):
    ins, outs = refs[: count + 2], refs[count + 2 : 2 * count + 3]
    q_ref, sems = refs[-2:]
    pack_ref = outs[-1]
    rows = q_ref.shape[0]
    pairs = [*zip(ins[:count], outs[:count])]
    pairs += [(ins[count], q_ref), (ins[count + 1], pack_ref.at[pl.ds(rows, rows)])]
    fetch(pairs, sems)
    pack_ref[:rows, :] = q_ref[...] * jnp.bfloat16(inv_temp)


def prep_kernel(
    n_batch, ids_ref, logq_ref, counts_ref, bias_ref, weight_ref, wcol_ref
):
    own = lax.axis_index("batch")
    first_block = lax.axis_index("mem") * n_batch
    reqs = counts_ref.shape[0] * LANES
    sub = lax.broadcasted_iota(jnp.int32, (reqs, LANES), 0)
    lane = lax.broadcasted_iota(jnp.int32, (reqs, LANES), 1)
    ones = jnp.ones((LANES, LANES), jnp.bfloat16)
    ends = jnp.zeros((reqs, LANES), jnp.float32)
    for c in range(counts_ref.shape[0]):
        part = counts_ref[c : c + 1, :].astype(jnp.float32)
        tri = jnp.where(lane + c * LANES <= sub, part, 0.0).astype(jnp.bfloat16)
        ends = ends + jnp.dot(tri, ones, preferred_element_type=jnp.float32)
    ends = ends.astype(jnp.int32)
    sub = sub[:LANES]
    lane = lane[:LANES]
    rows = []
    for k in range(n_batch):
        block = first_block + jnp.bitwise_xor(own, k)
        pos = block * LANES + lane[:1]
        done = ends <= pos
        start = jnp.max(jnp.where(done, ends, 0), axis=0, keepdims=True)
        end = jnp.min(jnp.where(done, jnp.int32(2**30), ends), axis=0, keepdims=True)
        weight = 1.0 / (end - start).astype(jnp.float32)
        weight_ref[k : k + 1, :] = weight
        if k == 0:
            wcol_ref[...] = as_column(weight)
        rows.append((ids_ref[pl.ds(block, 1), :], start))
    for n in range(n_batch):
        block = first_block + jnp.bitwise_xor(own, n)
        id_col, start_col = as_column(rows[n][0]), as_column(rows[n][1])
        shift_col = as_column(-logq_ref[pl.ds(block, 1), :].astype(jnp.float32) * logq_unit)
        for k in range(n_batch):
            id_row, start = rows[k]
            keep = (id_col != id_row) & (start_col != start)
            if n == k:
                keep = keep | (sub == lane)
            bias_ref[n * LANES : (n + 1) * LANES, k * LANES : (k + 1) * LANES] = jnp.where(
                keep, shift_col, very_low
            )


def bank_kernel(
    n_batch, order, pack_ref, s0, s1, s2, s3, ids_ref, mem_ids_ref, mem_logq_ref, mem_age_ref,
    bank_ref, logit_ref, lse_ref,
):
    own = lax.axis_index("batch")
    group = lax.axis_index("mem")
    slots = s0.shape[0]
    for k, shard in zip((0, *order), (s0, s1, s2, s3)):
        at = pl.multiple_of(jnp.bitwise_xor(group, k) * slots, slots)
        bank_ref[pl.ds(at, slots), :] = shard[...]
    id_row = ids_ref[pl.ds(group * n_batch + own, 1), :]
    id_col = as_column(mem_ids_ref[pl.ds(own, 1), :])
    shift_col = as_column(-mem_logq_ref[pl.ds(own, 1), :].astype(jnp.float32) * logq_unit)
    age_col = as_column(mem_age_ref[pl.ds(own, 1), :])
    keep = (age_col < AGE_LIMIT) & (id_col != id_row)
    bias = jnp.where(keep, shift_col, very_low)
    logit = nt_dot(bank_ref[...], pack_ref[:LANES, :]) + bias
    top = jnp.max(logit, axis=0, keepdims=True)
    total = jnp.sum(jnp.exp(logit - top), axis=0, keepdims=True)
    logit_ref[...] = logit
    lse_ref[...] = top + jnp.log(total)


def order_kernel(order, *refs):
    for k, ref in zip(order, refs[:-1]):
        refs[-1][k // 2 : k // 2 + 1, :] = ref[...]


def stack_kernel(*refs):
    first = 0
    for ref in refs[:-1]:
        refs[-1][first : first + ref.shape[0], :] = ref[...]
        first += ref.shape[0]


def stats_kernel(n_batch, *refs):
    evens = refs[: n_batch // 2]
    odd_ref, odd_last_ref, bias_ref, queries, items, own_ref, row_ref, top_ref, total_ref = refs[
        n_batch // 2 :
    ]
    block = evens[0].shape[0]
    for k in range(n_batch // 2):
        odd = odd_last_ref if k == n_batch // 2 - 1 else odd_ref.at[pl.ds(k * block, block)]
        for parity, ref in enumerate((evens[k], odd)):
            at = (2 * k + parity) * LANES
            queries[at : at + LANES, :] = ref[:LANES, :]
            items[at : at + LANES, :] = ref[LANES:, :]
    width = 2 * LANES
    for c in range(n_batch // 2):
        at = slice(c * width, (c + 1) * width)
        logit = nt_dot(items[...], queries[at, :]) + bias_ref[:, at]
        top = jnp.max(logit, axis=0, keepdims=True)
        top_ref[:, at] = top
        total_ref[:, at] = jnp.sum(jnp.exp(logit - top), axis=0, keepdims=True)
        own_ref[:, at] = logit[:LANES]
        if c == 0:
            row_ref[...] = logit[:, :LANES]


def grad_kernel(
    n_batch, queries, items, own_ref, row_ref, top_ref, total_ref, even_ref, odd_ref,
    weight_ref, wcol_ref, bank_ref, mem_logit_ref, loss_ref, qgrad_ref, pgrad_ref,
):
    width = 2 * LANES
    pgrad = -wcol_ref[:, :1] * queries[:LANES, :].astype(jnp.float32)
    for c in range(n_batch // 2):
        at = slice(c * width, (c + 1) * width)
        top = top_ref[:, at]
        mem_lse = jnp.concatenate([even_ref[c : c + 1, :], odd_ref[c : c + 1, :]], axis=1)
        weight = jnp.concatenate(
            [weight_ref[2 * c : 2 * c + 1, :], weight_ref[2 * c + 1 : 2 * c + 2, :]], axis=1
        )
        high = jnp.maximum(top, mem_lse)
        lse = high + jnp.log(total_ref[:, at] * jnp.exp(top - high) + jnp.exp(mem_lse - high))
        coef = (weight * jnp.exp(own_ref[:, at] - lse)).astype(jnp.bfloat16)
        pgrad = pgrad + jnp.dot(coef, queries[at, :], preferred_element_type=jnp.float32)
        if c == 0:
            own_lse = lse[:, :LANES]
            own_weight = weight[:, :LANES]
            diag = lax.broadcasted_iota(jnp.int32, (LANES, LANES), 0) == (
                lax.broadcasted_iota(jnp.int32, (LANES, LANES), 1)
            )
            own_logit = jnp.sum(jnp.where(diag, row_ref[:LANES, :], 0.0), axis=0, keepdims=True)
            loss_ref[...] = own_lse - own_logit
            row_coef = (own_weight * jnp.exp(row_ref[...] - own_lse)).astype(jnp.bfloat16)
            mem_coef = (own_weight * jnp.exp(mem_logit_ref[...] - own_lse)).astype(jnp.bfloat16)
            qgrad = tn_dot(row_coef, items[...]) + tn_dot(mem_coef, bank_ref[...])
            qgrad_ref[...] = inv_temp * (
                qgrad - wcol_ref[:, :1] * items[:LANES, :].astype(jnp.float32)
            )
    pgrad_ref[...] = pgrad


def call(kernel, outs, args, hbm=(), scratch=(), cost_us=1):
    in_vmem = pl.BlockSpec(memory_space=pltpu.VMEM)
    in_hbm = pl.BlockSpec(memory_space=pltpu.HBM)
    args = [
        pltpu.with_memory_space_constraint(a, pltpu.HBM) if k in hbm else a
        for k, a in enumerate(args)
    ]
    return pl.pallas_call(
        kernel,
        out_shape=outs,
        in_specs=[in_hbm if k in hbm else in_vmem for k in range(len(args))],
        out_specs=[in_vmem] * len(outs),
        scratch_shapes=list(scratch),
        compiler_params=pltpu.CompilerParams(vmem_limit_bytes=VMEM_LIMIT),
        cost_estimate=pl.CostEstimate(
            flops=int(cost_us * 1e9), bytes_accessed=int(cost_us * 3e6), transcendentals=0
        ),
    )(*args)


def f32(*shape):
    return jax.ShapeDtypeStruct(shape, jnp.float32)


def bf16(*shape):
    return jax.ShapeDtypeStruct(shape, jnp.bfloat16)


def swap(array, axis, mask):
    size = lax.axis_size(axis)
    return lax.ppermute(array, axis, [(s, s ^ mask) for s in range(size)])


def after(array, *others):
    return lax.optimization_barrier((array, *others))[0]


def small_body(
    queries, positives, pos_ids, pos_logq, mem_items, mem_ids, mem_logq, mem_age, counts
):
    own_count, depth = queries.shape
    n_batch = lax.axis_size("batch")
    group_rows = own_count * n_batch
    ints = [
        a.reshape(-1, LANES) for a in (pos_ids, pos_logq, counts, mem_ids, mem_logq, mem_age)
    ]

    small = (*ints, mem_items)
    *ints, shard, pack = call(
        lambda *r: pack_kernel(len(small), *r),
        [jax.ShapeDtypeStruct(a.shape, a.dtype) for a in small] + [bf16(2 * own_count, depth)],
        (*small, queries, positives),
        hbm=range(len(small) + 2),
        scratch=[
            pltpu.VMEM(queries.shape, queries.dtype),
            pltpu.SemaphoreType.DMA((len(small) + 2,)),
        ],
    )
    far = swap(pack, "batch", 4)
    near = swap(pack, "batch", 2)
    arrived = {k: swap(shard, "mem", k) for k in BANK_ORDER}
    shards = [shard] + [arrived[k] for k in BANK_ORDER]
    bias, weight, wcol = call(
        lambda *r: prep_kernel(n_batch, *r),
        [f32(group_rows, group_rows), f32(n_batch, LANES), f32(LANES, LANES)],
        ints[:3],
        cost_us=3,
    )
    bank, mem_logit, lse = call(
        lambda *r: bank_kernel(n_batch, BANK_ORDER, *r),
        [bf16(LANES, depth), f32(LANES, LANES), f32(1, LANES)],
        (pack, *shards, ints[0], *ints[3:]),
    )
    last = swap(far, "batch", 2)
    sums = {k: swap(lse, "batch", k) for k in SUM_ORDER}
    (even,) = call(
        lambda *r: order_kernel((0, *SUM_ORDER), *r),
        [f32(4, LANES)],
        [lse] + [sums[k] for k in SUM_ORDER],
    )
    odd = swap(after(even, weight), "batch", 1)
    (early,) = call(stack_kernel, [bf16(6 * own_count, depth)], (pack, near, far))
    odd_early = swap(early, "batch", 1)
    odd_last = swap(last, "batch", 1)
    stats = call(
        lambda *r: stats_kernel(n_batch, *r),
        [bf16(group_rows, depth), bf16(group_rows, depth), f32(own_count, group_rows)]
        + [f32(group_rows, own_count), f32(1, group_rows), f32(1, group_rows)],
        (pack, near, far, last, odd_early, odd_last, bias),
        cost_us=3,
    )
    loss, query_grad, positive_grad = call(
        lambda *r: grad_kernel(n_batch, *r),
        [f32(1, LANES), f32(own_count, depth), f32(own_count, depth)],
        (*stats, even, odd, weight, wcol, bank, mem_logit),
        cost_us=1,
    )
    return loss.reshape(own_count), query_grad, positive_grad


def request_span(counts, positions):
    ends = jnp.cumsum(counts)
    which = jnp.searchsorted(ends, positions, side="right")
    return which, jnp.take(counts, which)


def masked_exp(tile_logits, level):
    return jnp.where(tile_logits > very_low, jnp.exp(tile_logits - level[:, None]), 0.0)


def large_body(
    queries, positives, pos_ids, pos_logq, mem_items, mem_ids, mem_logq, mem_age, counts
):
    own_count = queries.shape[0]
    group_rows = own_count * lax.axis_size("batch")
    bank_rows = mem_items.shape[0] * lax.axis_size("mem")
    batch_index = lax.axis_index("batch")
    group_first = lax.axis_index("mem") * group_rows
    own_first = group_first + batch_index * own_count
    bank_first = batch_index * bank_rows

    def part(array, first, size):
        return lax.dynamic_slice_in_dim(array, first, size, 0)

    def shift_of(array, first, size):
        return -part(array, first, size).astype(jnp.float32) * logq_unit

    own_rows = own_first + jnp.arange(own_count, dtype=jnp.int32)
    col_rows = group_first + jnp.arange(group_rows, dtype=jnp.int32)
    own_req, own_size = request_span(counts, own_rows)
    weight = 1.0 / own_size.astype(jnp.float32)
    cand_req, _ = request_span(counts, col_rows)
    own_ids = part(pos_ids, own_first, own_count)
    cand_ids = part(pos_ids, group_first, group_rows)
    bank_ids = part(mem_ids, bank_first, bank_rows)
    bank_live = part(mem_age, bank_first, bank_rows) < AGE_LIMIT
    bank_items = lax.all_gather(mem_items, "mem", axis=0, tiled=True)
    mem_mask = bank_live[None, :] & (bank_ids[None, :] != own_ids[:, None])
    mem_logits = jnp.where(
        mem_mask,
        inv_temp * nt_dot(queries, bank_items) + shift_of(mem_logq, bank_first, bank_rows)[None, :],
        very_low,
    )
    group_items = lax.all_gather(positives, "batch", axis=0, tiled=True)
    kept = (col_rows[None, :] == own_rows[:, None]) | (
        cand_ids[None, :] != own_ids[:, None]
    ) & (cand_req[None, :] != own_req[:, None])
    logits = jnp.where(
        kept,
        inv_temp * nt_dot(queries, group_items)
        + shift_of(pos_logq, group_first, group_rows)[None, :],
        very_low,
    )
    row_max = jnp.maximum(jnp.max(logits, axis=1), jnp.max(mem_logits, axis=1))
    row_lse = row_max + jnp.log(
        jnp.sum(masked_exp(logits, row_max), axis=1)
        + jnp.sum(masked_exp(mem_logits, row_max), axis=1)
    )
    pos_coef = (weight[:, None] * masked_exp(logits, row_lse)).astype(jnp.bfloat16)
    mem_coef = (weight[:, None] * masked_exp(mem_logits, row_lse)).astype(jnp.bfloat16)
    own_term = inv_temp * weight[:, None]
    query_grad = inv_temp * (
        jnp.dot(pos_coef, group_items, preferred_element_type=jnp.float32)
        + jnp.dot(mem_coef, bank_items, preferred_element_type=jnp.float32)
    ) - own_term * positives.astype(jnp.float32)
    column_share = lax.psum_scatter(
        inv_temp * tn_dot(pos_coef, queries), "batch", scatter_dimension=0, tiled=True
    )
    wide_q = queries.astype(jnp.float32)
    own_logit = inv_temp * jnp.sum(wide_q * positives.astype(jnp.float32), axis=1) + shift_of(
        pos_logq, own_first, own_count
    )
    return row_lse - own_logit, query_grad, column_share - own_term * wide_q


def solution(mesh):
    small = mesh.shape["batch"] == 8 and mesh.shape["mem"] == 4
    own = P(("mem", "batch"), None)
    in_specs = (own, own, P(), P(), P(("batch", "mem"), None), P(), P(), P(), P())
    out_specs = (P(("mem", "batch")), own, own)
    return jax.shard_map(
        small_body if small else large_body,
        mesh=mesh,
        in_specs=in_specs,
        out_specs=out_specs,
        check_vma=False,
    )
```

```python
import jax
import jax.numpy as jnp
from jax import lax
from jax.experimental import pallas as pl
from jax.experimental.pallas import tpu as pltpu
from jax.sharding import PartitionSpec as P

AGE_LIMIT = 16
inv_temp = 8.0
logq_unit = 1.0 / 1024.0
very_low = -1e30
LANES = 128
VMEM_LIMIT = 32 * 1024 * 1024
BANK_ORDER = (3, 1, 2)
SUM_ORDER = (6, 4, 2)


def nt_dot(left_mat, right_mat):
    return lax.dot_general(
        left_mat, right_mat, (((1,), (1,)), ((), ())), preferred_element_type=jnp.float32
    )


def tn_dot(left_mat, right_mat):
    return lax.dot_general(
        left_mat, right_mat, (((0,), (0,)), ((), ())), preferred_element_type=jnp.float32
    )


def as_column(row):
    return jnp.broadcast_to(row, (LANES, LANES)).T


def fetch(pairs, sems):
    copies = [pltpu.make_async_copy(src, dst, sems.at[k]) for k, (src, dst) in enumerate(pairs)]
    for copy in copies:
        copy.start()
    for copy in copies:
        copy.wait()


def pack_kernel(count, *refs):
    ins, outs = refs[: count + 2], refs[count + 2 : 2 * count + 3]
    q_ref, sems = refs[-2:]
    pack_ref = outs[-1]
    rows = q_ref.shape[0]
    pairs = [(ins[count], q_ref), (ins[count + 1], pack_ref.at[pl.ds(rows, rows)])]
    pairs += [*zip(ins[:count], outs[:count])]
    fetch(pairs, sems)
    pack_ref[:rows, :] = q_ref[...] * jnp.bfloat16(inv_temp)


def prep_kernel(
    n_batch, ids_ref, logq_ref, counts_ref, bias_ref, weight_ref, wcol_ref
):
    own = lax.axis_index("batch")
    first_block = lax.axis_index("mem") * n_batch
    reqs = counts_ref.shape[0] * LANES
    sub = lax.broadcasted_iota(jnp.int32, (reqs, LANES), 0)
    lane = lax.broadcasted_iota(jnp.int32, (reqs, LANES), 1)
    ones = jnp.ones((LANES, LANES), jnp.bfloat16)
    ends = jnp.zeros((reqs, LANES), jnp.float32)
    for c in range(counts_ref.shape[0]):
        part = counts_ref[c : c + 1, :].astype(jnp.float32)
        tri = jnp.where(lane + c * LANES <= sub, part, 0.0).astype(jnp.bfloat16)
        ends = ends + jnp.dot(tri, ones, preferred_element_type=jnp.float32)
    sub = sub[:LANES]
    lane = lane[:LANES]
    rows = []
    for k in range(n_batch):
        block = first_block + jnp.bitwise_xor(own, k)
        pos = (block * LANES + lane[:1]).astype(jnp.float32)
        done = ends <= pos
        start = jnp.max(jnp.where(done, ends, 0.0), axis=0, keepdims=True)
        end = jnp.min(jnp.where(done, -very_low, ends), axis=0, keepdims=True)
        weight = 1.0 / (end - start)
        weight_ref[k : k + 1, :] = weight
        if k == 0:
            wcol_ref[...] = as_column(weight)
        rows.append((ids_ref[pl.ds(block, 1), :], start))
    for n in range(n_batch):
        block = first_block + jnp.bitwise_xor(own, n)
        id_col, start_col = as_column(rows[n][0]), as_column(rows[n][1])
        shift_col = as_column(-logq_ref[pl.ds(block, 1), :].astype(jnp.float32) * logq_unit)
        for k in range(n_batch):
            id_row, start = rows[k]
            keep = (id_col != id_row) & (start_col != start)
            if n == k:
                keep = keep | (sub == lane)
            bias_ref[n * LANES : (n + 1) * LANES, k * LANES : (k + 1) * LANES] = jnp.where(
                keep, shift_col, very_low
            )


def bank_kernel(
    n_batch, order, pack_ref, s0, s1, s2, s3, ids_ref, mem_ids_ref, mem_logq_ref, mem_age_ref,
    bank_ref, logit_ref, lse_ref,
):
    own = lax.axis_index("batch")
    group = lax.axis_index("mem")
    slots = s0.shape[0]
    for k, shard in zip((0, *order), (s0, s1, s2, s3)):
        at = pl.multiple_of(jnp.bitwise_xor(group, k) * slots, slots)
        bank_ref[pl.ds(at, slots), :] = shard[...]
    id_row = ids_ref[pl.ds(group * n_batch + own, 1), :]
    id_col = as_column(mem_ids_ref[pl.ds(own, 1), :])
    shift_col = as_column(-mem_logq_ref[pl.ds(own, 1), :].astype(jnp.float32) * logq_unit)
    age_col = as_column(mem_age_ref[pl.ds(own, 1), :])
    keep = (age_col < AGE_LIMIT) & (id_col != id_row)
    bias = jnp.where(keep, shift_col, very_low)
    logit = nt_dot(bank_ref[...], pack_ref[:LANES, :]) + bias
    top = jnp.max(logit, axis=0, keepdims=True)
    total = jnp.sum(jnp.exp(logit - top), axis=0, keepdims=True)
    logit_ref[...] = logit
    lse_ref[...] = top + jnp.log(total)


def order_kernel(order, *refs):
    for k, ref in zip(order, refs[:-1]):
        refs[-1][k // 2 : k // 2 + 1, :] = ref[...]


def stack_kernel(*refs):
    first = 0
    for ref in refs[:-1]:
        refs[-1][first : first + ref.shape[0], :] = ref[...]
        first += ref.shape[0]


def stats_kernel(n_batch, *refs):
    evens = refs[: n_batch // 2]
    odd_ref, odd_last_ref, bias_ref = refs[n_batch // 2 : n_batch // 2 + 3]
    queries, items, own_ref, pull_ref, top_ref, total_ref, diag_ref = refs[n_batch // 2 + 3 :]
    block = evens[0].shape[0]
    for k in range(n_batch // 2):
        odd = odd_last_ref if k == n_batch // 2 - 1 else odd_ref.at[pl.ds(k * block, block)]
        for parity, ref in enumerate((evens[k], odd)):
            at = (2 * k + parity) * LANES
            queries[at : at + LANES, :] = ref[:LANES, :]
            items[at : at + LANES, :] = ref[LANES:, :]
    logit = nt_dot(items[...], queries[...]) + bias_ref[...]
    top = jnp.max(logit, axis=0, keepdims=True)
    exps = jnp.exp(logit - top)
    top_ref[...] = top
    total_ref[...] = jnp.sum(exps, axis=0, keepdims=True)
    own_ref[...] = exps[:LANES]
    pull_ref[...] = tn_dot(exps[:, :LANES].astype(jnp.bfloat16), items[...])
    diag = lax.broadcasted_iota(jnp.int32, (LANES, LANES), 0) == (
        lax.broadcasted_iota(jnp.int32, (LANES, LANES), 1)
    )
    diag_ref[...] = jnp.sum(
        jnp.where(diag, logit[:LANES, :LANES], 0.0), axis=0, keepdims=True
    )


def grad_kernel(
    n_batch, queries, items, own_ref, pull_ref, top_ref, total_ref, diag_ref, even_ref, odd_ref,
    weight_ref, wcol_ref, bank_ref, mem_logit_ref, loss_ref, qgrad_ref, pgrad_ref,
):
    def in_line(even, odd):
        return [ref[c : c + 1, :] for c in range(n_batch // 2) for ref in (even, odd)]

    mem_lse = jnp.concatenate(in_line(even_ref, odd_ref), axis=1)
    weight = jnp.concatenate([weight_ref[k : k + 1, :] for k in range(n_batch)], axis=1)
    top = top_ref[...]
    high = jnp.maximum(top, mem_lse)
    below = jnp.exp(top - high)
    lse = high + jnp.log(total_ref[...] * below + jnp.exp(mem_lse - high))
    scale = weight * jnp.exp(top - lse)
    own_lse = lse[:, :LANES]
    loss_ref[...] = own_lse - diag_ref[...]
    weight_col = wcol_ref[:, :1]
    mem_coef = (weight[:, :LANES] * jnp.exp(mem_logit_ref[...] - own_lse)).astype(jnp.bfloat16)
    pull = as_column(scale[:, :LANES])[:, :1] * pull_ref[...] + tn_dot(mem_coef, bank_ref[...])
    qgrad_ref[...] = inv_temp * (pull - weight_col * items[:LANES, :].astype(jnp.float32))
    coef = (own_ref[...] * scale).astype(jnp.bfloat16)
    pgrad = jnp.dot(coef, queries[...], preferred_element_type=jnp.float32)
    pgrad_ref[...] = pgrad - weight_col * queries[:LANES, :].astype(jnp.float32)


def call(kernel, outs, args, hbm=(), scratch=(), cost_us=1):
    in_vmem = pl.BlockSpec(memory_space=pltpu.VMEM)
    in_hbm = pl.BlockSpec(memory_space=pltpu.HBM)
    args = [
        pltpu.with_memory_space_constraint(a, pltpu.HBM) if k in hbm else a
        for k, a in enumerate(args)
    ]
    return pl.pallas_call(
        kernel,
        out_shape=outs,
        in_specs=[in_hbm if k in hbm else in_vmem for k in range(len(args))],
        out_specs=[in_vmem] * len(outs),
        scratch_shapes=list(scratch),
        compiler_params=pltpu.CompilerParams(vmem_limit_bytes=VMEM_LIMIT),
        cost_estimate=pl.CostEstimate(
            flops=int(cost_us * 1e9), bytes_accessed=int(cost_us * 3e6), transcendentals=0
        ),
    )(*args)


def f32(*shape):
    return jax.ShapeDtypeStruct(shape, jnp.float32)


def bf16(*shape):
    return jax.ShapeDtypeStruct(shape, jnp.bfloat16)


def swap(array, axis, mask):
    size = lax.axis_size(axis)
    return lax.ppermute(array, axis, [(s, s ^ mask) for s in range(size)])


def after(array, *others):
    return lax.optimization_barrier((array, *others))[0]


def small_body(
    queries, positives, pos_ids, pos_logq, mem_items, mem_ids, mem_logq, mem_age, counts
):
    own_count, depth = queries.shape
    n_batch = lax.axis_size("batch")
    group_rows = own_count * n_batch
    ints = [
        a.reshape(-1, LANES) for a in (pos_ids, pos_logq, counts, mem_ids, mem_logq, mem_age)
    ]

    small = (*ints, mem_items)
    *ints, shard, pack = call(
        lambda *r: pack_kernel(len(small), *r),
        [jax.ShapeDtypeStruct(a.shape, a.dtype) for a in small] + [bf16(2 * own_count, depth)],
        (*small, queries, positives),
        hbm=range(len(small) + 2),
        scratch=[
            pltpu.VMEM(queries.shape, queries.dtype),
            pltpu.SemaphoreType.DMA((len(small) + 2,)),
        ],
    )
    far = swap(pack, "batch", 4)
    near = swap(pack, "batch", 2)
    arrived = {k: swap(shard, "mem", k) for k in BANK_ORDER}
    shards = [shard] + [arrived[k] for k in BANK_ORDER]
    bias, weight, wcol = call(
        lambda *r: prep_kernel(n_batch, *r),
        [f32(group_rows, group_rows), f32(n_batch, LANES), f32(LANES, LANES)],
        ints[:3],
        cost_us=3,
    )
    bank, mem_logit, lse = call(
        lambda *r: bank_kernel(n_batch, BANK_ORDER, *r),
        [bf16(LANES, depth), f32(LANES, LANES), f32(1, LANES)],
        (pack, *shards, ints[0], *ints[3:]),
    )
    last = swap(far, "batch", 2)
    sums = {k: swap(lse, "batch", k) for k in SUM_ORDER}
    (even,) = call(
        lambda *r: order_kernel((0, *SUM_ORDER), *r),
        [f32(4, LANES)],
        [lse] + [sums[k] for k in SUM_ORDER],
    )
    odd = swap(after(even, weight), "batch", 1)
    (early,) = call(stack_kernel, [bf16(6 * own_count, depth)], (pack, near, far))
    odd_early = swap(early, "batch", 1)
    odd_last = swap(last, "batch", 1)
    stats = call(
        lambda *r: stats_kernel(n_batch, *r),
        [bf16(group_rows, depth), bf16(group_rows, depth), f32(own_count, group_rows)]
        + [f32(own_count, depth), f32(1, group_rows), f32(1, group_rows), f32(1, LANES)],
        (pack, near, far, last, odd_early, odd_last, bias),
        cost_us=3,
    )
    loss, query_grad, positive_grad = call(
        lambda *r: grad_kernel(n_batch, *r),
        [f32(1, LANES), f32(own_count, depth), f32(own_count, depth)],
        (*stats, even, odd, weight, wcol, bank, mem_logit),
        cost_us=1,
    )
    return loss.reshape(own_count), query_grad, positive_grad


def request_span(counts, positions):
    ends = jnp.cumsum(counts)
    which = jnp.searchsorted(ends, positions, side="right")
    return which, jnp.take(counts, which)


def masked_exp(tile_logits, level):
    return jnp.where(tile_logits > very_low, jnp.exp(tile_logits - level[:, None]), 0.0)


def large_body(
    queries, positives, pos_ids, pos_logq, mem_items, mem_ids, mem_logq, mem_age, counts
):
    own_count = queries.shape[0]
    group_rows = own_count * lax.axis_size("batch")
    bank_rows = mem_items.shape[0] * lax.axis_size("mem")
    batch_index = lax.axis_index("batch")
    group_first = lax.axis_index("mem") * group_rows
    own_first = group_first + batch_index * own_count
    bank_first = batch_index * bank_rows

    def part(array, first, size):
        return lax.dynamic_slice_in_dim(array, first, size, 0)

    def shift_of(array, first, size):
        return -part(array, first, size).astype(jnp.float32) * logq_unit

    own_rows = own_first + jnp.arange(own_count, dtype=jnp.int32)
    col_rows = group_first + jnp.arange(group_rows, dtype=jnp.int32)
    own_req, own_size = request_span(counts, own_rows)
    weight = 1.0 / own_size.astype(jnp.float32)
    cand_req, _ = request_span(counts, col_rows)
    own_ids = part(pos_ids, own_first, own_count)
    cand_ids = part(pos_ids, group_first, group_rows)
    bank_ids = part(mem_ids, bank_first, bank_rows)
    bank_live = part(mem_age, bank_first, bank_rows) < AGE_LIMIT
    bank_items = lax.all_gather(mem_items, "mem", axis=0, tiled=True)
    mem_mask = bank_live[None, :] & (bank_ids[None, :] != own_ids[:, None])
    mem_logits = jnp.where(
        mem_mask,
        inv_temp * nt_dot(queries, bank_items) + shift_of(mem_logq, bank_first, bank_rows)[None, :],
        very_low,
    )
    group_items = lax.all_gather(positives, "batch", axis=0, tiled=True)
    kept = (col_rows[None, :] == own_rows[:, None]) | (
        cand_ids[None, :] != own_ids[:, None]
    ) & (cand_req[None, :] != own_req[:, None])
    logits = jnp.where(
        kept,
        inv_temp * nt_dot(queries, group_items)
        + shift_of(pos_logq, group_first, group_rows)[None, :],
        very_low,
    )
    row_max = jnp.maximum(jnp.max(logits, axis=1), jnp.max(mem_logits, axis=1))
    row_lse = row_max + jnp.log(
        jnp.sum(masked_exp(logits, row_max), axis=1)
        + jnp.sum(masked_exp(mem_logits, row_max), axis=1)
    )
    pos_coef = (weight[:, None] * masked_exp(logits, row_lse)).astype(jnp.bfloat16)
    mem_coef = (weight[:, None] * masked_exp(mem_logits, row_lse)).astype(jnp.bfloat16)
    own_term = inv_temp * weight[:, None]
    query_grad = inv_temp * (
        jnp.dot(pos_coef, group_items, preferred_element_type=jnp.float32)
        + jnp.dot(mem_coef, bank_items, preferred_element_type=jnp.float32)
    ) - own_term * positives.astype(jnp.float32)
    column_share = lax.psum_scatter(
        inv_temp * tn_dot(pos_coef, queries), "batch", scatter_dimension=0, tiled=True
    )
    wide_q = queries.astype(jnp.float32)
    own_logit = inv_temp * jnp.sum(wide_q * positives.astype(jnp.float32), axis=1) + shift_of(
        pos_logq, own_first, own_count
    )
    return row_lse - own_logit, query_grad, column_share - own_term * wide_q


def solution(mesh):
    small = mesh.shape["batch"] == 8 and mesh.shape["mem"] == 4
    own = P(("mem", "batch"), None)
    in_specs = (own, own, P(), P(), P(("batch", "mem"), None), P(), P(), P(), P())
    out_specs = (P(("mem", "batch")), own, own)
    return jax.shard_map(
        small_body if small else large_body,
        mesh=mesh,
        in_specs=in_specs,
        out_specs=out_specs,
        check_vma=False,
    )
```

```python
import jax
import jax.numpy as jnp
from jax import lax
from jax.experimental import pallas as pl
from jax.experimental.pallas import tpu as pltpu
from jax.sharding import PartitionSpec as P

AGE_LIMIT = 16
inv_temp = 8.0
logq_unit = 1.0 / 1024.0
very_low = -1e30
LANES = 128
VMEM_LIMIT = 32 * 1024 * 1024
BANK_ORDER = (3, 1, 2)
SUM_ORDER = (6, 4, 2)


def nt_dot(left_mat, right_mat):
    return lax.dot_general(
        left_mat, right_mat, (((1,), (1,)), ((), ())), preferred_element_type=jnp.float32
    )


def tn_dot(left_mat, right_mat):
    return lax.dot_general(
        left_mat, right_mat, (((0,), (0,)), ((), ())), preferred_element_type=jnp.float32
    )


def as_column(row):
    return jnp.broadcast_to(row, (LANES, LANES)).T


def fetch(pairs, sems):
    copies = [pltpu.make_async_copy(src, dst, sems.at[k]) for k, (src, dst) in enumerate(pairs)]
    for copy in copies:
        copy.start()
    for copy in copies:
        copy.wait()


def pack_kernel(count, *refs):
    ins, outs = refs[: count + 2], refs[count + 2 : 2 * count + 3]
    q_ref, sems = refs[-2:]
    pack_ref = outs[-1]
    rows = q_ref.shape[0]
    pairs = [(ins[count], q_ref), (ins[count + 1], pack_ref.at[pl.ds(rows, rows)])]
    pairs += [*zip(ins[:count], outs[:count])]
    fetch(pairs, sems)
    pack_ref[:rows, :] = q_ref[...] * jnp.bfloat16(inv_temp)


def prep_kernel(
    n_batch, ids_ref, logq_ref, counts_ref, bias_ref, weight_ref, wcol_ref
):
    own = lax.axis_index("batch")
    first_block = lax.axis_index("mem") * n_batch
    reqs = counts_ref.shape[0] * LANES
    sub = lax.broadcasted_iota(jnp.int32, (reqs, LANES), 0)
    lane = lax.broadcasted_iota(jnp.int32, (reqs, LANES), 1)
    ones = jnp.ones((LANES, LANES), jnp.bfloat16)
    ends = jnp.zeros((reqs, LANES), jnp.float32)
    for c in range(counts_ref.shape[0]):
        part = counts_ref[c : c + 1, :].astype(jnp.float32)
        tri = jnp.where(lane + c * LANES <= sub, part, 0.0).astype(jnp.bfloat16)
        ends = ends + jnp.dot(tri, ones, preferred_element_type=jnp.float32)
    sub = sub[:LANES]
    lane = lane[:LANES]
    rows = []
    for k in range(n_batch):
        block = first_block + jnp.bitwise_xor(own, k)
        pos = (block * LANES + lane[:1]).astype(jnp.float32)
        done = ends <= pos
        start = jnp.max(jnp.where(done, ends, 0.0), axis=0, keepdims=True)
        end = jnp.min(jnp.where(done, -very_low, ends), axis=0, keepdims=True)
        weight = 1.0 / (end - start)
        weight_ref[k : k + 1, :] = weight
        if k == 0:
            wcol_ref[...] = as_column(weight)
        rows.append((ids_ref[pl.ds(block, 1), :], start))
    for n in range(n_batch):
        block = first_block + jnp.bitwise_xor(own, n)
        id_col, start_col = as_column(rows[n][0]), as_column(rows[n][1])
        shift_col = as_column(-logq_ref[pl.ds(block, 1), :].astype(jnp.float32) * logq_unit)
        for k in range(n_batch):
            id_row, start = rows[k]
            keep = (id_col != id_row) & (start_col != start)
            if n == k:
                keep = keep | (sub == lane)
            bias_ref[n * LANES : (n + 1) * LANES, k * LANES : (k + 1) * LANES] = jnp.where(
                keep, shift_col, very_low
            )


def bank_kernel(
    n_batch, order, pack_ref, s0, s1, s2, s3, ids_ref, mem_ids_ref, mem_logq_ref, mem_age_ref,
    bank_ref, logit_ref, lse_ref,
):
    own = lax.axis_index("batch")
    group = lax.axis_index("mem")
    slots = s0.shape[0]
    for k, shard in zip((0, *order), (s0, s1, s2, s3)):
        at = pl.multiple_of(jnp.bitwise_xor(group, k) * slots, slots)
        bank_ref[pl.ds(at, slots), :] = shard[...]
    id_row = ids_ref[pl.ds(group * n_batch + own, 1), :]
    id_col = as_column(mem_ids_ref[pl.ds(own, 1), :])
    shift_col = as_column(-mem_logq_ref[pl.ds(own, 1), :].astype(jnp.float32) * logq_unit)
    age_col = as_column(mem_age_ref[pl.ds(own, 1), :])
    keep = (age_col < AGE_LIMIT) & (id_col != id_row)
    bias = jnp.where(keep, shift_col, very_low)
    logit = nt_dot(bank_ref[...], pack_ref[:LANES, :]) + bias
    top = jnp.max(logit, axis=0, keepdims=True)
    total = jnp.sum(jnp.exp(logit - top), axis=0, keepdims=True)
    logit_ref[...] = logit
    lse_ref[...] = top + jnp.log(total)


def order_kernel(order, *refs):
    for k, ref in zip(order, refs[:-1]):
        refs[-1][k // 2 : k // 2 + 1, :] = ref[...]


def stack_kernel(*refs):
    first = 0
    for ref in refs[:-1]:
        refs[-1][first : first + ref.shape[0], :] = ref[...]
        first += ref.shape[0]


def stats_kernel(places, *refs):
    count = 1 + max(operand for operand, _, _ in places)
    bias_ref, queries, items, own_ref, pull_ref, top_ref, total_ref, diag_ref = refs[count:]
    for operand, first, k in places:
        at = slice(k * LANES, (k + 1) * LANES)
        queries[at, :] = refs[operand][first : first + LANES, :]
        items[at, :] = refs[operand][first + LANES : first + 2 * LANES, :]
    logit = nt_dot(items[...], queries[...]) + bias_ref[...]
    top = jnp.max(logit, axis=0, keepdims=True)
    exps = jnp.exp(logit - top)
    top_ref[...] = top
    total_ref[...] = jnp.sum(exps, axis=0, keepdims=True)
    own_ref[...] = exps[:LANES]
    pull_ref[...] = tn_dot(exps[:, :LANES].astype(jnp.bfloat16), items[...])
    diag = lax.broadcasted_iota(jnp.int32, (LANES, LANES), 0) == (
        lax.broadcasted_iota(jnp.int32, (LANES, LANES), 1)
    )
    diag_ref[...] = jnp.sum(
        jnp.where(diag, logit[:LANES, :LANES], 0.0), axis=0, keepdims=True
    )


def grad_kernel(
    n_batch, queries, items, own_ref, pull_ref, top_ref, total_ref, diag_ref, even_ref, odd_ref,
    weight_ref, wcol_ref, bank_ref, mem_logit_ref, loss_ref, qgrad_ref, pgrad_ref,
):
    def in_line(even, odd):
        return [ref[c : c + 1, :] for c in range(n_batch // 2) for ref in (even, odd)]

    mem_lse = jnp.concatenate(in_line(even_ref, odd_ref), axis=1)
    weight = jnp.concatenate([weight_ref[k : k + 1, :] for k in range(n_batch)], axis=1)
    top = top_ref[...]
    high = jnp.maximum(top, mem_lse)
    below = jnp.exp(top - high)
    lse = high + jnp.log(total_ref[...] * below + jnp.exp(mem_lse - high))
    scale = weight * jnp.exp(top - lse)
    own_lse = lse[:, :LANES]
    loss_ref[...] = own_lse - diag_ref[...]
    weight_col = wcol_ref[:, :1]
    mem_coef = (weight[:, :LANES] * jnp.exp(mem_logit_ref[...] - own_lse)).astype(jnp.bfloat16)
    pull = as_column(scale[:, :LANES])[:, :1] * pull_ref[...] + tn_dot(mem_coef, bank_ref[...])
    qgrad_ref[...] = inv_temp * (pull - weight_col * items[:LANES, :].astype(jnp.float32))
    coef = (own_ref[...] * scale).astype(jnp.bfloat16)
    pgrad = jnp.dot(coef, queries[...], preferred_element_type=jnp.float32)
    pgrad_ref[...] = pgrad - weight_col * queries[:LANES, :].astype(jnp.float32)


def call(kernel, outs, args, hbm=(), scratch=(), cost_us=1):
    in_vmem = pl.BlockSpec(memory_space=pltpu.VMEM)
    in_hbm = pl.BlockSpec(memory_space=pltpu.HBM)
    args = [
        pltpu.with_memory_space_constraint(a, pltpu.HBM) if k in hbm else a
        for k, a in enumerate(args)
    ]
    return pl.pallas_call(
        kernel,
        out_shape=outs,
        in_specs=[in_hbm if k in hbm else in_vmem for k in range(len(args))],
        out_specs=[in_vmem] * len(outs),
        scratch_shapes=list(scratch),
        compiler_params=pltpu.CompilerParams(vmem_limit_bytes=VMEM_LIMIT),
        cost_estimate=pl.CostEstimate(
            flops=int(cost_us * 1e9), bytes_accessed=int(cost_us * 3e6), transcendentals=0
        ),
    )(*args)


def f32(*shape):
    return jax.ShapeDtypeStruct(shape, jnp.float32)


def bf16(*shape):
    return jax.ShapeDtypeStruct(shape, jnp.bfloat16)


def swap(array, axis, mask):
    size = lax.axis_size(axis)
    return lax.ppermute(array, axis, [(s, s ^ mask) for s in range(size)])


def after(array, *others):
    return lax.optimization_barrier((array, *others))[0]


def small_body(
    queries, positives, pos_ids, pos_logq, mem_items, mem_ids, mem_logq, mem_age, counts
):
    own_count, depth = queries.shape
    n_batch = lax.axis_size("batch")
    group_rows = own_count * n_batch
    ints = [
        a.reshape(-1, LANES) for a in (pos_ids, pos_logq, counts, mem_ids, mem_logq, mem_age)
    ]

    small = (*ints, mem_items)
    *ints, shard, pack = call(
        lambda *r: pack_kernel(len(small), *r),
        [jax.ShapeDtypeStruct(a.shape, a.dtype) for a in small] + [bf16(2 * own_count, depth)],
        (*small, queries, positives),
        hbm=range(len(small) + 2),
        scratch=[
            pltpu.VMEM(queries.shape, queries.dtype),
            pltpu.SemaphoreType.DMA((len(small) + 2,)),
        ],
    )
    far = swap(pack, "batch", 4)
    arrived = {k: swap(shard, "mem", k) for k in BANK_ORDER}
    shards = [shard] + [arrived[k] for k in BANK_ORDER]
    near = swap(after(pack, arrived[2]), "batch", 2)
    bias, weight, wcol = call(
        lambda *r: prep_kernel(n_batch, *r),
        [f32(group_rows, group_rows), f32(n_batch, LANES), f32(LANES, LANES)],
        ints[:3],
        cost_us=3,
    )
    bank, mem_logit, lse = call(
        lambda *r: bank_kernel(n_batch, BANK_ORDER, *r),
        [bf16(LANES, depth), f32(LANES, LANES), f32(1, LANES)],
        (pack, *shards, ints[0], *ints[3:]),
    )
    last = swap(far, "batch", 2)
    sums = {k: swap(lse, "batch", k) for k in SUM_ORDER}
    (even,) = call(
        lambda *r: order_kernel((0, *SUM_ORDER), *r),
        [f32(4, LANES)],
        [lse] + [sums[k] for k in SUM_ORDER],
    )
    odd = swap(even, "batch", 1)
    block = pack.shape[0]
    pair = [bf16(2 * block, depth)]
    odd_early = swap(call(stack_kernel, pair, (pack, far))[0], "batch", 1)
    odd_late = swap(call(stack_kernel, pair, (near, last))[0], "batch", 1)
    places = [(0, 0, 0), (1, 0, 2), (2, 0, 4), (3, 0, 6)]
    places += [(4, 0, 1), (4, block, 5), (5, 0, 3), (5, block, 7)]
    stats = call(
        lambda *r: stats_kernel(places, *r),
        [bf16(group_rows, depth), bf16(group_rows, depth), f32(own_count, group_rows)]
        + [f32(own_count, depth), f32(1, group_rows), f32(1, group_rows), f32(1, LANES)],
        (pack, near, far, last, odd_early, odd_late, bias),
        cost_us=3,
    )
    loss, query_grad, positive_grad = call(
        lambda *r: grad_kernel(n_batch, *r),
        [f32(1, LANES), f32(own_count, depth), f32(own_count, depth)],
        (*stats, even, odd, weight, wcol, bank, mem_logit),
        cost_us=1,
    )
    return loss.reshape(own_count), query_grad, positive_grad


def request_span(counts, positions):
    ends = jnp.cumsum(counts)
    which = jnp.searchsorted(ends, positions, side="right")
    return which, jnp.take(counts, which)


def masked_exp(tile_logits, level):
    return jnp.where(tile_logits > very_low, jnp.exp(tile_logits - level[:, None]), 0.0)


def large_body(
    queries, positives, pos_ids, pos_logq, mem_items, mem_ids, mem_logq, mem_age, counts
):
    own_count = queries.shape[0]
    group_rows = own_count * lax.axis_size("batch")
    bank_rows = mem_items.shape[0] * lax.axis_size("mem")
    batch_index = lax.axis_index("batch")
    group_first = lax.axis_index("mem") * group_rows
    own_first = group_first + batch_index * own_count
    bank_first = batch_index * bank_rows

    def part(array, first, size):
        return lax.dynamic_slice_in_dim(array, first, size, 0)

    def shift_of(array, first, size):
        return -part(array, first, size).astype(jnp.float32) * logq_unit

    own_rows = own_first + jnp.arange(own_count, dtype=jnp.int32)
    col_rows = group_first + jnp.arange(group_rows, dtype=jnp.int32)
    own_req, own_size = request_span(counts, own_rows)
    weight = 1.0 / own_size.astype(jnp.float32)
    cand_req, _ = request_span(counts, col_rows)
    own_ids = part(pos_ids, own_first, own_count)
    cand_ids = part(pos_ids, group_first, group_rows)
    bank_ids = part(mem_ids, bank_first, bank_rows)
    bank_live = part(mem_age, bank_first, bank_rows) < AGE_LIMIT
    bank_items = lax.all_gather(mem_items, "mem", axis=0, tiled=True)
    mem_mask = bank_live[None, :] & (bank_ids[None, :] != own_ids[:, None])
    mem_logits = jnp.where(
        mem_mask,
        inv_temp * nt_dot(queries, bank_items) + shift_of(mem_logq, bank_first, bank_rows)[None, :],
        very_low,
    )
    group_items = lax.all_gather(positives, "batch", axis=0, tiled=True)
    kept = (col_rows[None, :] == own_rows[:, None]) | (
        cand_ids[None, :] != own_ids[:, None]
    ) & (cand_req[None, :] != own_req[:, None])
    logits = jnp.where(
        kept,
        inv_temp * nt_dot(queries, group_items)
        + shift_of(pos_logq, group_first, group_rows)[None, :],
        very_low,
    )
    row_max = jnp.maximum(jnp.max(logits, axis=1), jnp.max(mem_logits, axis=1))
    row_lse = row_max + jnp.log(
        jnp.sum(masked_exp(logits, row_max), axis=1)
        + jnp.sum(masked_exp(mem_logits, row_max), axis=1)
    )
    pos_coef = (weight[:, None] * masked_exp(logits, row_lse)).astype(jnp.bfloat16)
    mem_coef = (weight[:, None] * masked_exp(mem_logits, row_lse)).astype(jnp.bfloat16)
    own_term = inv_temp * weight[:, None]
    query_grad = inv_temp * (
        jnp.dot(pos_coef, group_items, preferred_element_type=jnp.float32)
        + jnp.dot(mem_coef, bank_items, preferred_element_type=jnp.float32)
    ) - own_term * positives.astype(jnp.float32)
    column_share = lax.psum_scatter(
        inv_temp * tn_dot(pos_coef, queries), "batch", scatter_dimension=0, tiled=True
    )
    wide_q = queries.astype(jnp.float32)
    own_logit = inv_temp * jnp.sum(wide_q * positives.astype(jnp.float32), axis=1) + shift_of(
        pos_logq, own_first, own_count
    )
    return row_lse - own_logit, query_grad, column_share - own_term * wide_q


def solution(mesh):
    small = mesh.shape["batch"] == 8 and mesh.shape["mem"] == 4
    own = P(("mem", "batch"), None)
    in_specs = (own, own, P(), P(), P(("batch", "mem"), None), P(), P(), P(), P())
    out_specs = (P(("mem", "batch")), own, own)
    return jax.shard_map(
        small_body if small else large_body,
        mesh=mesh,
        in_specs=in_specs,
        out_specs=out_specs,
        check_vma=False,
    )
```

```python
import jax
import jax.numpy as jnp
from jax import lax
from jax.experimental import pallas as pl
from jax.experimental.pallas import tpu as pltpu
from jax.sharding import PartitionSpec as P

AGE_LIMIT = 16
inv_temp = 8.0
logq_unit = 1.0 / 1024.0
very_low = -1e30
LANES = 128
VMEM_LIMIT = 32 * 1024 * 1024
BANK_ORDER = (3, 1, 2)
SUM_ORDER = (6, 4, 2)


def nt_dot(left_mat, right_mat):
    return lax.dot_general(
        left_mat, right_mat, (((1,), (1,)), ((), ())), preferred_element_type=jnp.float32
    )


def tn_dot(left_mat, right_mat):
    return lax.dot_general(
        left_mat, right_mat, (((0,), (0,)), ((), ())), preferred_element_type=jnp.float32
    )


def as_column(row):
    return jnp.broadcast_to(row, (LANES, LANES)).T


def pack_kernel(count, *refs):
    ins, outs = refs[: count + 2], refs[count + 2 : 2 * count + 3]
    q_ref, sems = refs[-2:]
    pack_ref = outs[-1]
    rows = q_ref.shape[0]
    pairs = [(ins[count], q_ref), (ins[count + 1], pack_ref.at[pl.ds(rows, rows)])]
    pairs += [*zip(ins[:count], outs[:count])]
    copies = [pltpu.make_async_copy(src, dst, sems.at[k]) for k, (src, dst) in enumerate(pairs)]
    for copy in copies:
        copy.start()
    copies[0].wait()
    pack_ref[:rows, :] = q_ref[...] * jnp.bfloat16(inv_temp)
    for copy in copies[1:]:
        copy.wait()


def prep_kernel(
    n_batch, ids_ref, logq_ref, counts_ref, bias_ref, weight_ref, wcol_ref
):
    own = lax.axis_index("batch")
    first_block = lax.axis_index("mem") * n_batch
    reqs = counts_ref.shape[0] * LANES
    sub = lax.broadcasted_iota(jnp.int32, (reqs, LANES), 0)
    lane = lax.broadcasted_iota(jnp.int32, (reqs, LANES), 1)
    ones = jnp.ones((LANES, LANES), jnp.bfloat16)
    ends = jnp.zeros((reqs, LANES), jnp.float32)
    for c in range(counts_ref.shape[0]):
        part = counts_ref[c : c + 1, :].astype(jnp.float32)
        tri = jnp.where(lane + c * LANES <= sub, part, 0.0).astype(jnp.bfloat16)
        ends = ends + jnp.dot(tri, ones, preferred_element_type=jnp.float32)
    sub = sub[:LANES]
    lane = lane[:LANES]
    rows = []
    for k in range(n_batch):
        block = first_block + jnp.bitwise_xor(own, k)
        pos = (block * LANES + lane[:1]).astype(jnp.float32)
        done = ends <= pos
        start = jnp.max(jnp.where(done, ends, 0.0), axis=0, keepdims=True)
        end = jnp.min(jnp.where(done, -very_low, ends), axis=0, keepdims=True)
        weight = 1.0 / (end - start)
        weight_ref[k : k + 1, :] = weight
        if k == 0:
            wcol_ref[...] = as_column(weight)
        rows.append((ids_ref[pl.ds(block, 1), :], start))
    for n in range(n_batch):
        block = first_block + jnp.bitwise_xor(own, n)
        id_col, start_col = as_column(rows[n][0]), as_column(rows[n][1])
        shift_col = as_column(-logq_ref[pl.ds(block, 1), :].astype(jnp.float32) * logq_unit)
        for k in range(n_batch):
            id_row, start = rows[k]
            keep = (id_col != id_row) & (start_col != start)
            if n == k:
                keep = keep | (sub == lane)
            bias_ref[n * LANES : (n + 1) * LANES, k * LANES : (k + 1) * LANES] = jnp.where(
                keep, shift_col, very_low
            )


def bank_kernel(
    n_batch, order, pack_ref, s0, s1, s2, s3, ids_ref, mem_ids_ref, mem_logq_ref, mem_age_ref,
    bank_ref, logit_ref, lse_ref,
):
    own = lax.axis_index("batch")
    group = lax.axis_index("mem")
    slots = s0.shape[0]
    for k, shard in zip((0, *order), (s0, s1, s2, s3)):
        at = pl.multiple_of(jnp.bitwise_xor(group, k) * slots, slots)
        bank_ref[pl.ds(at, slots), :] = shard[...]
    id_row = ids_ref[pl.ds(group * n_batch + own, 1), :]
    id_col = as_column(mem_ids_ref[pl.ds(own, 1), :])
    shift_col = as_column(-mem_logq_ref[pl.ds(own, 1), :].astype(jnp.float32) * logq_unit)
    age_col = as_column(mem_age_ref[pl.ds(own, 1), :])
    keep = (age_col < AGE_LIMIT) & (id_col != id_row)
    bias = jnp.where(keep, shift_col, very_low)
    logit = nt_dot(bank_ref[...], pack_ref[:LANES, :]) + bias
    top = jnp.max(logit, axis=0, keepdims=True)
    total = jnp.sum(jnp.exp(logit - top), axis=0, keepdims=True)
    logit_ref[...] = logit
    lse_ref[...] = top + jnp.log(total)


def order_kernel(order, *refs):
    for k, ref in zip(order, refs[:-1]):
        refs[-1][k // 2 : k // 2 + 1, :] = ref[...]


def stack_kernel(*refs):
    first = 0
    for ref in refs[:-1]:
        refs[-1][first : first + ref.shape[0], :] = ref[...]
        first += ref.shape[0]


def stats_kernel(places, *refs):
    count = 1 + max(operand for operand, _, _ in places)
    bias_ref, queries, items, own_ref, pull_ref, top_ref, total_ref, diag_ref = refs[count:]
    for operand, first, k in places:
        at = slice(k * LANES, (k + 1) * LANES)
        queries[at, :] = refs[operand][first : first + LANES, :]
        items[at, :] = refs[operand][first + LANES : first + 2 * LANES, :]
    logit = nt_dot(items[...], queries[...]) + bias_ref[...]
    top = jnp.max(logit, axis=0, keepdims=True)
    exps = jnp.exp(logit - top)
    top_ref[...] = top
    total_ref[...] = jnp.sum(exps, axis=0, keepdims=True)
    own_ref[...] = exps[:LANES]
    pull_ref[...] = tn_dot(exps[:, :LANES].astype(jnp.bfloat16), items[...])
    diag = lax.broadcasted_iota(jnp.int32, (LANES, LANES), 0) == (
        lax.broadcasted_iota(jnp.int32, (LANES, LANES), 1)
    )
    diag_ref[...] = jnp.sum(
        jnp.where(diag, logit[:LANES, :LANES], 0.0), axis=0, keepdims=True
    )


def grad_kernel(
    n_batch, queries, items, own_ref, pull_ref, top_ref, total_ref, diag_ref, even_ref, odd_ref,
    weight_ref, wcol_ref, bank_ref, mem_logit_ref, loss_ref, qgrad_ref, pgrad_ref,
):
    def in_line(even, odd):
        return [ref[c : c + 1, :] for c in range(n_batch // 2) for ref in (even, odd)]

    mem_lse = jnp.concatenate(in_line(even_ref, odd_ref), axis=1)
    weight = jnp.concatenate([weight_ref[k : k + 1, :] for k in range(n_batch)], axis=1)
    top = top_ref[...]
    high = jnp.maximum(top, mem_lse)
    below = jnp.exp(top - high)
    lse = high + jnp.log(total_ref[...] * below + jnp.exp(mem_lse - high))
    scale = weight * jnp.exp(top - lse)
    own_lse = lse[:, :LANES]
    loss_ref[...] = own_lse - diag_ref[...]
    weight_col = wcol_ref[:, :1]
    mem_coef = (weight[:, :LANES] * jnp.exp(mem_logit_ref[...] - own_lse)).astype(jnp.bfloat16)
    pull = as_column(scale[:, :LANES])[:, :1] * pull_ref[...] + tn_dot(mem_coef, bank_ref[...])
    qgrad_ref[...] = inv_temp * (pull - weight_col * items[:LANES, :].astype(jnp.float32))
    coef = (own_ref[...] * scale).astype(jnp.bfloat16)
    pgrad = jnp.dot(coef, queries[...], preferred_element_type=jnp.float32)
    pgrad_ref[...] = pgrad - weight_col * queries[:LANES, :].astype(jnp.float32)


def call(kernel, outs, args, hbm=(), scratch=(), cost_us=1):
    in_vmem = pl.BlockSpec(memory_space=pltpu.VMEM)
    in_hbm = pl.BlockSpec(memory_space=pltpu.HBM)
    args = [
        pltpu.with_memory_space_constraint(a, pltpu.HBM) if k in hbm else a
        for k, a in enumerate(args)
    ]
    return pl.pallas_call(
        kernel,
        out_shape=outs,
        in_specs=[in_hbm if k in hbm else in_vmem for k in range(len(args))],
        out_specs=[in_vmem] * len(outs),
        scratch_shapes=list(scratch),
        compiler_params=pltpu.CompilerParams(vmem_limit_bytes=VMEM_LIMIT),
        cost_estimate=pl.CostEstimate(
            flops=int(cost_us * 1e9), bytes_accessed=int(cost_us * 3e6), transcendentals=0
        ),
    )(*args)


def f32(*shape):
    return jax.ShapeDtypeStruct(shape, jnp.float32)


def bf16(*shape):
    return jax.ShapeDtypeStruct(shape, jnp.bfloat16)


def swap(array, axis, mask):
    size = lax.axis_size(axis)
    return lax.ppermute(array, axis, [(s, s ^ mask) for s in range(size)])


def after(array, *others):
    return lax.optimization_barrier((array, *others))[0]


def small_body(
    queries, positives, pos_ids, pos_logq, mem_items, mem_ids, mem_logq, mem_age, counts
):
    own_count, depth = queries.shape
    n_batch = lax.axis_size("batch")
    group_rows = own_count * n_batch
    ints = [
        a.reshape(-1, LANES) for a in (pos_ids, pos_logq, counts, mem_ids, mem_logq, mem_age)
    ]

    small = (*ints, mem_items)
    *ints, shard, pack = call(
        lambda *r: pack_kernel(len(small), *r),
        [jax.ShapeDtypeStruct(a.shape, a.dtype) for a in small] + [bf16(2 * own_count, depth)],
        (*small, queries, positives),
        hbm=range(len(small) + 2),
        scratch=[
            pltpu.VMEM(queries.shape, queries.dtype),
            pltpu.SemaphoreType.DMA((len(small) + 2,)),
        ],
    )
    far = swap(pack, "batch", 4)
    arrived = {k: swap(shard, "mem", k) for k in BANK_ORDER}
    shards = [shard] + [arrived[k] for k in BANK_ORDER]
    near = swap(after(pack, arrived[2]), "batch", 2)
    bias, weight, wcol = call(
        lambda *r: prep_kernel(n_batch, *r),
        [f32(group_rows, group_rows), f32(n_batch, LANES), f32(LANES, LANES)],
        ints[:3],
        cost_us=3,
    )
    bank, mem_logit, lse = call(
        lambda *r: bank_kernel(n_batch, BANK_ORDER, *r),
        [bf16(LANES, depth), f32(LANES, LANES), f32(1, LANES)],
        (pack, *shards, ints[0], *ints[3:]),
    )
    last = swap(far, "batch", 2)
    sums = {k: swap(lse, "batch", k) for k in SUM_ORDER}
    (even,) = call(
        lambda *r: order_kernel((0, *SUM_ORDER), *r),
        [f32(4, LANES)],
        [lse] + [sums[k] for k in SUM_ORDER],
    )
    odd = swap(even, "batch", 1)
    block = pack.shape[0]
    pair = [bf16(2 * block, depth)]
    odd_early = swap(call(stack_kernel, pair, (pack, far))[0], "batch", 1)
    odd_late = swap(call(stack_kernel, pair, (near, last))[0], "batch", 1)
    places = [(0, 0, 0), (1, 0, 2), (2, 0, 4), (3, 0, 6)]
    places += [(4, 0, 1), (4, block, 5), (5, 0, 3), (5, block, 7)]
    stats = call(
        lambda *r: stats_kernel(places, *r),
        [bf16(group_rows, depth), bf16(group_rows, depth), f32(own_count, group_rows)]
        + [f32(own_count, depth), f32(1, group_rows), f32(1, group_rows), f32(1, LANES)],
        (pack, near, far, last, odd_early, odd_late, bias),
        cost_us=3,
    )
    loss, query_grad, positive_grad = call(
        lambda *r: grad_kernel(n_batch, *r),
        [f32(1, LANES), f32(own_count, depth), f32(own_count, depth)],
        (*stats, even, odd, weight, wcol, bank, mem_logit),
        cost_us=1,
    )
    return loss.reshape(own_count), query_grad, positive_grad


def request_span(counts, positions):
    ends = jnp.cumsum(counts)
    which = jnp.searchsorted(ends, positions, side="right")
    return which, jnp.take(counts, which)


def masked_exp(tile_logits, level):
    return jnp.where(tile_logits > very_low, jnp.exp(tile_logits - level[:, None]), 0.0)


def large_body(
    queries, positives, pos_ids, pos_logq, mem_items, mem_ids, mem_logq, mem_age, counts
):
    own_count = queries.shape[0]
    group_rows = own_count * lax.axis_size("batch")
    bank_rows = mem_items.shape[0] * lax.axis_size("mem")
    batch_index = lax.axis_index("batch")
    group_first = lax.axis_index("mem") * group_rows
    own_first = group_first + batch_index * own_count
    bank_first = batch_index * bank_rows

    def part(array, first, size):
        return lax.dynamic_slice_in_dim(array, first, size, 0)

    def shift_of(array, first, size):
        return -part(array, first, size).astype(jnp.float32) * logq_unit

    own_rows = own_first + jnp.arange(own_count, dtype=jnp.int32)
    col_rows = group_first + jnp.arange(group_rows, dtype=jnp.int32)
    own_req, own_size = request_span(counts, own_rows)
    weight = 1.0 / own_size.astype(jnp.float32)
    cand_req, _ = request_span(counts, col_rows)
    own_ids = part(pos_ids, own_first, own_count)
    cand_ids = part(pos_ids, group_first, group_rows)
    bank_ids = part(mem_ids, bank_first, bank_rows)
    bank_live = part(mem_age, bank_first, bank_rows) < AGE_LIMIT
    bank_items = lax.all_gather(mem_items, "mem", axis=0, tiled=True)
    mem_mask = bank_live[None, :] & (bank_ids[None, :] != own_ids[:, None])
    mem_logits = jnp.where(
        mem_mask,
        inv_temp * nt_dot(queries, bank_items) + shift_of(mem_logq, bank_first, bank_rows)[None, :],
        very_low,
    )
    group_items = lax.all_gather(positives, "batch", axis=0, tiled=True)
    kept = (col_rows[None, :] == own_rows[:, None]) | (
        cand_ids[None, :] != own_ids[:, None]
    ) & (cand_req[None, :] != own_req[:, None])
    logits = jnp.where(
        kept,
        inv_temp * nt_dot(queries, group_items)
        + shift_of(pos_logq, group_first, group_rows)[None, :],
        very_low,
    )
    row_max = jnp.maximum(jnp.max(logits, axis=1), jnp.max(mem_logits, axis=1))
    row_lse = row_max + jnp.log(
        jnp.sum(masked_exp(logits, row_max), axis=1)
        + jnp.sum(masked_exp(mem_logits, row_max), axis=1)
    )
    pos_coef = (weight[:, None] * masked_exp(logits, row_lse)).astype(jnp.bfloat16)
    mem_coef = (weight[:, None] * masked_exp(mem_logits, row_lse)).astype(jnp.bfloat16)
    own_term = inv_temp * weight[:, None]
    query_grad = inv_temp * (
        jnp.dot(pos_coef, group_items, preferred_element_type=jnp.float32)
        + jnp.dot(mem_coef, bank_items, preferred_element_type=jnp.float32)
    ) - own_term * positives.astype(jnp.float32)
    column_share = lax.psum_scatter(
        inv_temp * tn_dot(pos_coef, queries), "batch", scatter_dimension=0, tiled=True
    )
    wide_q = queries.astype(jnp.float32)
    own_logit = inv_temp * jnp.sum(wide_q * positives.astype(jnp.float32), axis=1) + shift_of(
        pos_logq, own_first, own_count
    )
    return row_lse - own_logit, query_grad, column_share - own_term * wide_q


def solution(mesh):
    small = mesh.shape["batch"] == 8 and mesh.shape["mem"] == 4
    own = P(("mem", "batch"), None)
    in_specs = (own, own, P(), P(), P(("batch", "mem"), None), P(), P(), P(), P())
    out_specs = (P(("mem", "batch")), own, own)
    return jax.shard_map(
        small_body if small else large_body,
        mesh=mesh,
        in_specs=in_specs,
        out_specs=out_specs,
        check_vma=False,
    )
```
